256 devices in a mesh: lev: 8 (over y, core), lat: 32 (over z, x).
Axes of the slice: x: 4, y: 4, z: 8, core: 2. Of those that a mesh axis runs over, the one named last changes fastest.
Arguments:
- tracer_mass: bfloat16 [48, 16, 192, 512], P(None, 'lev', 'lat'), may hold values from -6 to 6
- level_wind: bfloat16 [16, 192, 512], P('lev', 'lat'), may hold values from -0.8984375 to 0.8984375
- east_wind: bfloat16 [16, 192, 512], P('lev', 'lat'), may hold values from -0.8984375 to 0.8984375
- north_wind: bfloat16 [16, 192, 512], P('lev', 'lat'), may hold values from -0.8984375 to 0.8984375
- photolysis: bfloat16 [16, 192, 512], P('lev', 'lat'), may hold values from 0.099609375 to 2
- rate_matrix: bfloat16 [48, 48], replicated, may hold values from -0.875 to 0.875
- loss_rate: float32 [48], replicated, may hold values from 0.2 to 4
- substeps: int32 [48], replicated, may hold values from 1 to 2, as said below
- slot_table: int32 [8, 48], P('lev'), may hold values from -1 to 63, as said below
Outputs:
- updated: bfloat16 [48, 16, 192, 512], P(None, 'lev', 'lat')
The draws below stay inside these ranges and needn't reach their ends.
Inputs may be any that keep to these rules, and one draw needn't show every extreme that they name: Some tracer takes exactly 2 substeps. `slot_table`: in each level group the non-negative entries are distinct; only whether an entry is non-negative enters the outputs; the starting program reads slot s as belonging to owner s // 2 of the lat axis, so under that reading an owner holds at most 2 tracers of a level group, and in every level group some owner holds exactly 2.
All inputs are finite; a program needn't handle non-finite values.
Results may differ from the reference program's by a relative error of at most 0.0055.
Values may be sent and summed in bfloat16 or wider, within the bound.
A program may use at most 64 MiB of HBM per device.

```python
import math
import jax
import jax.numpy as jnp
from jax import lax

TRACERS = 48
NLON = 512
L_DEV = 2
SUBMAX = 2
LEVELS = 16
NLAT = 192
LEV_GROUPS = 8
CAP = 2
SLOTS = 64


def draw_substeps(key, part):
    key = jax.random.fold_in(key, 11)
    first_key, second_key = jax.random.split(key)
    step_draw = jax.random.randint(first_key, (TRACERS,), 1, SUBMAX + 1)
    where_most = jax.random.randint(second_key, (), 0, TRACERS)
    return step_draw.at[where_most].set(SUBMAX).astype(jnp.int32)


def draw_slot_table(key, part):
    key = jax.random.fold_in(key, 23)

    def one_group(group_key):
        group_keys = jax.random.split(group_key, 4)
        owner_count = SLOTS // CAP
        full_owner = jax.random.randint(group_keys[0], (), 0, owner_count)
        ranking = jax.random.permutation(group_keys[1], SLOTS)
        slot_owner = jnp.arange(SLOTS) // CAP
        scores = jnp.where(slot_owner == full_owner, ranking - SLOTS, ranking)
        ordered = jnp.argsort(scores, stable=True)[:TRACERS]
        shuffle = jax.random.permutation(group_keys[2], TRACERS)
        slot_of = jnp.zeros((TRACERS,), jnp.int32).at[shuffle].set(ordered.astype(jnp.int32))
        keeper = (jax.random.randint(group_keys[3], (TRACERS,), 0, 4) > 0) | (slot_of // CAP == full_owner)
        return jnp.where(keeper, slot_of, -1).astype(jnp.int32)
    return jax.vmap(one_group)(jax.random.split(key, LEV_GROUPS))


def steps_of(own_key, shape, shards, low, high):
    def one(axis_at, blocks):
        draws = jax.random.uniform(jax.random.fold_in(jax.random.fold_in(own_key, 6), axis_at), (blocks,), jnp.float32, low / len(shards), high / len(shards))
        return jnp.repeat(jnp.exp(draws), shape[axis_at] // blocks).reshape((-1,) + (1,) * (len(shape) - axis_at - 1))

    level = one(*shards[0])
    for cut in shards[1:]:
        level = level * one(*cut)
    return level


def bell_draw(key, dims, scale, bound, cuts=(), held_as=jnp.bfloat16):
    result = scale * jax.random.normal(key, dims, jnp.float32)
    if cuts:
        result = result * steps_of(key, dims, cuts, -0.22, 0.18)
    return jnp.clip(result, -bound, bound).astype(held_as)


def setup_inputs(seed: int = 0) -> dict:
    key_list = jax.random.split(jax.random.key(seed), 10)
    tracer_mass = bell_draw(key_list[0], (TRACERS, LEVELS, NLAT, NLON), 1.0, 6.0, ((1, 8), (2, 32)))
    level_wind = jnp.clip(jax.random.uniform(key_list[1], (LEVELS, NLAT, NLON), jnp.float32, -0.8984375, 0.8984375) * steps_of(key_list[1], (LEVELS, NLAT, NLON), ((0, 8), (1, 32)), -0.4, 0.0), -0.8984375, 0.8984375).astype(jnp.bfloat16)
    east_wind = jnp.clip(jax.random.uniform(key_list[2], (LEVELS, NLAT, NLON), jnp.float32, -0.8984375, 0.8984375) * steps_of(key_list[2], (LEVELS, NLAT, NLON), ((0, 8), (1, 32)), -0.4, 0.0), -0.8984375, 0.8984375).astype(jnp.bfloat16)
    north_wind = jnp.clip(jax.random.uniform(key_list[3], (LEVELS, NLAT, NLON), jnp.float32, -0.8984375, 0.8984375) * steps_of(key_list[3], (LEVELS, NLAT, NLON), ((0, 8), (1, 32)), -0.4, 0.0), -0.8984375, 0.8984375).astype(jnp.bfloat16)
    photolysis = jnp.clip(jnp.exp(math.log(2.0) - 2.9996462 * jax.random.uniform(key_list[4], (LEVELS, NLAT, NLON), jnp.float32) ** steps_of(key_list[4], (LEVELS, NLAT, NLON), ((0, 8), (1, 32)), -0.2, 0.2)), 0.099609375, 2.0).astype(jnp.bfloat16)
    rate_matrix = bell_draw(key_list[5], (TRACERS, TRACERS), TRACERS ** -0.5, 0.875)
    loss_rate = jnp.clip(jnp.exp(jax.random.uniform(key_list[6], (TRACERS,), jnp.float32, math.log(0.2), math.log(4.0))), 0.2, 4.0)
    substeps = draw_substeps(jax.random.fold_in(key_list[9], 71), 0)
    slot_table = draw_slot_table(jax.random.fold_in(key_list[9], 71), 0)
    return dict(tracer_mass=tracer_mass, level_wind=level_wind, east_wind=east_wind, north_wind=north_wind, photolysis=photolysis, rate_matrix=rate_matrix, loss_rate=loss_rate, substeps=substeps, slot_table=slot_table)


CHEM_DT = 0.5


def minmod(first_diff, second_diff):
    return 0.5 * (jnp.sign(first_diff) + jnp.sign(second_diff)) * jnp.minimum(jnp.abs(first_diff), jnp.abs(second_diff))


def face_flux(courant, lower_value, lower_slope, upper_value, upper_slope):
    return jnp.where(courant > 0.0, courant * (lower_value + 0.5 * (1.0 - courant) * lower_slope), courant * (upper_value - 0.5 * (1.0 + courant) * upper_slope))


def shaped(vector, from_end):
    return vector.reshape((-1,) + (1,) * (-from_end - 1))


def limited_sweep(amounts, courant, from_end, offset, extent, bounded):
    sweep_dim = amounts.ndim + from_end
    cell_count = amounts.shape[sweep_dim] - 4

    def take_slice(source, start_at, stop_at):
        return lax.slice_in_dim(source, start_at, stop_at, axis=sweep_dim)

    differences = take_slice(amounts, 1, cell_count + 4) - take_slice(amounts, 0, cell_count + 3)
    slopes = minmod(take_slice(differences, 1, cell_count + 3), take_slice(differences, 0, cell_count + 2))
    if bounded:
        positions = offset - 1 + jnp.arange(cell_count + 2, dtype=jnp.int32)
        inside = (positions > 0) & (positions < extent - 1)
        slopes = jnp.where(shaped(inside, from_end), slopes, 0.0)
        face_index = offset + jnp.arange(cell_count + 1, dtype=jnp.int32)
        opened = (face_index > 0) & (face_index < extent)
        courant = jnp.where(shaped(opened, from_end), courant, 0.0)
    fluxes = face_flux(courant, take_slice(amounts, 1, cell_count + 2), take_slice(slopes, 0, cell_count + 1), take_slice(amounts, 2, cell_count + 3), take_slice(slopes, 1, cell_count + 2))
    return take_slice(amounts, 2, cell_count + 2) - (take_slice(fluxes, 1, cell_count + 1) - take_slice(fluxes, 0, cell_count))


def east_sweep(amounts, east_faces, counts):
    courant = east_faces / jnp.maximum(counts, 1.0)
    extended = jnp.concatenate([amounts[..., -2:], amounts, amounts[..., :2]], axis=-1)
    courant = courant + jnp.zeros_like(extended[..., 2:-2])
    wrapped = jnp.concatenate([courant, courant[..., :1]], axis=-1)
    return limited_sweep(extended, wrapped, -1, 0, 0, False)


def north_sweep(extended, north_faces, counts, offset, extent):
    courant = north_faces / jnp.maximum(counts, 1.0)
    return limited_sweep(extended, courant, -2, offset, extent, True)


def pad_rows(amounts):
    widths = [(0, 0)] * (amounts.ndim - 2) + [(2, 2), (0, 0)]
    return jnp.pad(amounts, widths)


def substep_loop(amounts, counts, east_faces, extend, north_faces, offset, extent):
    for substep in range(SUBMAX):
        advanced = east_sweep(amounts, east_faces, counts)
        advanced = north_sweep(extend(advanced), north_faces, counts, offset, extent)
        amounts = jnp.where(counts > substep, advanced, amounts)
    return amounts


def reference(tracer_mass, level_wind, east_wind, north_wind, photolysis, rate_matrix, loss_rate, substeps, slot_table):
    vertical_faces = jnp.concatenate([level_wind.astype(jnp.float32), jnp.zeros((1, NLAT, NLON), jnp.float32)], axis=0)

    def vertical(tracer):
        extended = jnp.pad(tracer.astype(jnp.float32), ((2, 2), (0, 0), (0, 0)))
        return limited_sweep(extended, vertical_faces, -3, 0, LEVELS, True).astype(jnp.bfloat16)

    moved_up = lax.map(vertical, tracer_mass)
    carried = jnp.repeat(slot_table >= 0, L_DEV, axis=0)
    counts = jnp.where(carried.T, substeps[:, None], 0).astype(jnp.float32)
    east_faces = east_wind.astype(jnp.float32)
    north_faces = jnp.concatenate([north_wind.astype(jnp.float32), jnp.zeros((LEVELS, 1, NLON), jnp.float32)], axis=1)

    def horizontal(members):
        tracer, level_counts = members
        amounts = substep_loop(tracer.astype(jnp.float32), level_counts[:, None, None], east_faces, pad_rows, north_faces, 0, NLAT)
        return amounts.astype(jnp.bfloat16)

    moved_side = lax.map(horizontal, (moved_up, counts))
    by_level = jnp.transpose(moved_side, (1, 0, 2, 3))

    def chemistry(members):
        level_slab, photo_slab = members
        values = level_slab.astype(jnp.float32)
        production = jnp.einsum("st,sab->tab", rate_matrix.astype(jnp.float32), values)
        photo_dt = CHEM_DT * photo_slab.astype(jnp.float32)
        return ((values + photo_dt * production) / (1.0 + photo_dt * loss_rate[:, None, None])).astype(jnp.bfloat16)

    updated = lax.map(chemistry, (by_level, photolysis))
    return jnp.transpose(updated, (1, 0, 2, 3))
```

```python
import functools

import jax
import jax.numpy as jnp
from jax import lax
from jax.experimental import pallas as pl
from jax.experimental.pallas import tpu as pltpu
from jax.sharding import PartitionSpec as P

MESH = pl.DeviceIdType.MESH
CHEM_DT = 0.5
LANES = 128
GROUPS = 3
UNIT = 16

F32, BF16 = jnp.float32, jnp.bfloat16


def minmod(a, b):
    return jnp.maximum(jnp.minimum(a, b), jnp.minimum(jnp.maximum(a, b), 0.0))


def face(c, w, lower, upper, lower_slope, upper_slope):
    upwind = c > 0.0
    return c * (
        jnp.where(upwind, lower, upper) + w * jnp.where(upwind, lower_slope, upper_slope)
    )


def lane_iota():
    return lax.broadcasted_iota(jnp.int32, (8, LANES), 1)


def from_west(chunks):
    rolled = [pltpu.roll(x, 1, 1) for x in chunks]
    first = lane_iota() == 0
    return [jnp.where(first, rolled[k - 1], rolled[k]) for k in range(len(chunks))]


def from_east(chunks):
    rolled = [pltpu.roll(x, LANES - 1, 1) for x in chunks]
    last = lane_iota() == LANES - 1
    n = len(chunks)
    return [jnp.where(last, rolled[(k + 1) % n], rolled[k]) for k in range(n)]


def east_sweep(f, c, w, inv):
    fm = from_west(f)
    d = [a - b for a, b in zip(f, fm)]
    s = [minmod(a, b) for a, b in zip(from_east(d), d)]
    sm = from_west(s)
    g = [face(*args) for args in zip(c, w, fm, f, sm, s)]
    return [a - inv * (up - lo) for a, up, lo in zip(f, from_east(g), g)]


def vertical_sweep(below, own, above, c_lo, w_lo, c_hi, w_hi, even):
    m1 = jnp.where(even, pltpu.roll(below, 7, 0), pltpu.roll(own, 1, 0))
    p1 = jnp.where(even, pltpu.roll(own, 7, 0), pltpu.roll(above, 1, 0))
    d1, d2, d3, d4 = m1 - below, own - m1, p1 - own, above - p1
    sm, s0, sp = minmod(d1, d2), minmod(d2, d3), minmod(d3, d4)
    return own - (face(c_hi, w_hi, own, p1, s0, sp) - face(c_lo, w_lo, m1, own, sm, s0))


def kernel(
    n_lev,
    n_lat,
    x_ref,
    lw_ref,
    ew_ref,
    nw_ref,
    ph_ref,
    rate_ref,
    loss_ref,
    steps_ref,
    slots_ref,
    out_ref,
    below,
    above,
    a_ref,
    b_ref,
    h_ref,
    send1,
    send2,
    halo1,
    halo2,
    lw_next,
    cv_lo,
    wv_lo,
    cv_hi,
    wv_hi,
    ce,
    he,
    we2,
    cn,
    hn,
    wn2,
    pd,
    columns,
    lev_send,
    lev_recv,
    lat_send,
    lat_recv,
    wind_send,
    wind_recv,
):
    rows, pairs, lon = x_ref.shape
    span = pairs // GROUPS
    units = span // UNIT
    chunks = lon // LANES
    lev, lat = lax.axis_index("lev"), lax.axis_index("lat")
    up, down = lax.rem(lev + 1, n_lev), lax.rem(lev + n_lev - 1, n_lev)
    north, south = lax.rem(lat + 1, n_lat), lax.rem(lat + n_lat - 1, n_lat)
    has_up, has_down = lev < n_lev - 1, lev > 0
    has_north, has_south = lat < n_lat - 1, lat > 0

    barrier = pltpu.get_barrier_semaphore()
    for to in ((up, lat), (down, lat), (lev, north), (lev, south)):
        pl.semaphore_signal(barrier, inc=1, device_id=to, device_id_type=MESH)

    def remote(src, dst, send_sem, recv_sem, to):
        return pltpu.make_async_remote_copy(
            src_ref=src,
            dst_ref=dst,
            send_sem=send_sem,
            recv_sem=recv_sem,
            device_id=to,
            device_id_type=MESH,
        )

    def wind_copies():
        return (
            (has_down, has_up, remote(lw_ref, lw_next, wind_send.at[0], wind_recv.at[0], (down, lat))),
            (
                has_south,
                has_north,
                remote(cn.at[0], cn.at[rows], wind_send.at[1], wind_recv.at[1], (lev, south)),
            ),
        )

    def lev_copy(direction, part, group):
        to = ((up, lat), (down, lat))[direction]
        where = pl.ds(2 * part, 2), pl.ds(group * span, span)
        return remote(
            x_ref.at[where],
            (below, above)[direction].at[where],
            lev_send.at[direction, part, group],
            lev_recv.at[direction, part, group],
            to,
        )

    def lat_copy(substep, direction, group):
        to = ((lev, south), (lev, north))[direction]
        where = pl.ds(2 * direction, 2), pl.ds(group * span, span)
        return remote(
            (send1, send2)[substep].at[where],
            (halo1, halo2)[substep].at[where],
            lat_send.at[substep, direction, group],
            lat_recv.at[substep, direction, group],
            to,
        )

    lev_can_send, lev_can_recv = (has_up, has_down), (has_down, has_up)
    lat_can_send, lat_can_recv = (has_south, has_north), (has_north, has_south)

    even = lax.broadcasted_iota(jnp.int32, (8, LANES), 0) % 2 == 0

    def pattern(ref, r):
        v = ref[r].astype(F32)
        return jnp.concatenate([v] * 4, axis=0)

    even_row = lax.broadcasted_iota(jnp.int32, (8, lon), 0) % 2 == 0

    def tables(r, _):
        c = pattern(nw_ref, r)
        c = jnp.where((r == 0) & ~has_south, 0.0, c)
        cn[r] = c
        c = pattern(ew_ref, r)
        half = jnp.where(c > 0.0, 0.5, -0.5)
        ce[r] = c
        he[r] = half
        we2[r] = half - 0.25 * c
        c = pattern(lw_ref, r)
        c = jnp.where(even_row & ~has_down, 0.0, c)
        cv_lo[r] = c
        wv_lo[r] = jnp.where(c > 0.0, 0.5, -0.5) - 0.5 * c
        pd[r] = CHEM_DT * pattern(ph_ref, r)
        return 0

    lax.fori_loop(0, rows, tables, 0)

    pair_of = lax.broadcasted_iota(jnp.int32, (pairs, pairs // 2), 0) // 2
    tracer_of = lax.broadcasted_iota(jnp.int32, (pairs, pairs // 2), 1)
    picks = pair_of == tracer_of

    def column(row):
        value = jnp.sum(jnp.where(picks, row, 0.0), axis=1, keepdims=True)
        return jnp.broadcast_to(value, (pairs, LANES))

    steps = steps_ref[...]
    carried = slots_ref[...] >= 0
    first = jnp.where(carried, jnp.where(steps > 1, 0.5, 1.0), 0.0)
    second = jnp.where(carried & (steps > 1), 0.5, 0.0)
    columns[0] = column(first)
    columns[1] = column(second)
    columns[2] = column(loss_ref[...])
    expand = picks.astype(BF16)
    spread = lax.dot_general(
        expand, rate_ref[...], (((1,), (1,)), ((), ())), preferred_element_type=F32
    ).astype(BF16)
    spread = lax.dot_general(
        spread, expand, (((1,), (1,)), ((), ())), preferred_element_type=F32
    )
    same = (
        lax.broadcasted_iota(jnp.int32, (pairs, pairs), 0) % 2
        == lax.broadcasted_iota(jnp.int32, (pairs, pairs), 1) % 2
    )
    rates = jnp.where(same, spread, 0.0).astype(BF16)

    pl.semaphore_wait(barrier, 4)
    for can_send, _, copy in wind_copies():

        @pl.when(can_send)
        def _():
            copy.start()

    for group in range(GROUPS):
        for part in (0, 2):
            for direction in range(2):

                @pl.when(lev_can_send[direction])
                def _():
                    lev_copy(direction, part, group).start()

    for group in range(GROUPS):
        for direction in range(2):

            @pl.when(lev_can_send[direction])
            def _():
                lev_copy(direction, 1, group).start()

    def all_units(body):
        lax.fori_loop(0, rows * (pairs // UNIT), body, 0)

    def halves(value):
        return value[:8], value[8:]

    @pl.when(~has_down)
    def _():
        def fill(i, _):
            r, at = i // (pairs // UNIT), pl.ds(pl.multiple_of(i % (pairs // UNIT) * UNIT, UNIT), UNIT)
            for k in range(chunks):
                here = r, at, pl.ds(k * LANES, LANES)
                parts = [jnp.where(even, v, pltpu.roll(v, 1, 0)) for v in halves(x_ref[here].astype(F32))]
                below[here] = jnp.concatenate(parts, axis=0).astype(BF16)
            return 0

        all_units(fill)

    @pl.when(~has_up)
    def _():
        def fill(i, _):
            r, at = i // (pairs // UNIT), pl.ds(pl.multiple_of(i % (pairs // UNIT) * UNIT, UNIT), UNIT)
            for k in range(chunks):
                here = r, at, pl.ds(k * LANES, LANES)
                parts = [jnp.where(even, pltpu.roll(v, 7, 0), v) for v in halves(x_ref[here].astype(F32))]
                above[here] = jnp.concatenate(parts, axis=0).astype(BF16)
            return 0

        all_units(fill)
        lw_next[...] = jnp.zeros(lw_next.shape, BF16)

    for at_edge, where in ((~has_north, 0), (~has_south, 2)):

        @pl.when(at_edge)
        def _():
            zero = jnp.zeros((2, pairs, lon), BF16)
            halo1[pl.ds(where, 2)] = zero
            halo2[pl.ds(where, 2)] = zero

    @pl.when(~has_north)
    def _():
        cn[rows] = jnp.zeros((8, lon), F32)

    for _, can_recv, copy in wind_copies():

        @pl.when(can_recv)
        def _():
            copy.wait_recv()

    def more_tables(r, _):
        mine, theirs = pattern(lw_ref, r), pattern(lw_next, r)
        c = jnp.where(even_row, pltpu.roll(mine, 7, 0), pltpu.roll(theirs, 1, 0))
        c = jnp.where(~even_row & ~has_up, 0.0, c)
        cv_hi[r] = c
        wv_hi[r] = jnp.where(c > 0.0, 0.5, -0.5) - 0.5 * c
        return 0

    lax.fori_loop(0, rows, more_tables, 0)

    def north_tables(r, _):
        c = cn[r]
        half = jnp.where(c > 0.0, 0.5, -0.5)
        hn[r] = half
        wn2[r] = half - 0.25 * c
        return 0

    lax.fori_loop(0, rows + 1, north_tables, 0)

    def lane(k):
        return pl.ds(k * LANES, LANES)

    def column_of(which, at):
        return columns[which, at, :]

    def first_sweeps(group, r, unit, slot):
        base = pl.multiple_of(group * span + unit * UNIT, UNIT)
        at = pl.ds(base, UNIT)
        swept = []
        for k in range(chunks):
            here = r, at, lane(k)
            lo, own, hi = (halves(ref[here].astype(F32)) for ref in (below, x_ref, above))
            tables_here = [ref[r, :, lane(k)] for ref in (cv_lo, wv_lo, cv_hi, wv_hi)]
            moved = [vertical_sweep(lo[h], own[h], hi[h], *tables_here, even) for h in range(2)]
            swept.append(jnp.concatenate(moved, axis=0).astype(BF16).astype(F32))
        c = [ce[r, :, lane(k)] for k in range(chunks)]
        half = [he[r, :, lane(k)] for k in range(chunks)]
        after = []
        for h in range(2):
            at_half = pl.ds(pl.multiple_of(base + 8 * h, 8), 8)
            inv = column_of(0, at_half)
            scale = 0.5 * inv
            w = [b - scale * a for a, b in zip(c, half)]
            result = east_sweep([halves(v)[h] for v in swept], c, w, inv)
            for k in range(chunks):
                a_ref[r, at_half, lane(k)] = result[k]
            after.append(result)
        if slot is not None:
            for k in range(chunks):
                both = jnp.concatenate([after[0][k], after[1][k]], axis=0)
                send1[slot, at, lane(k)] = both.astype(BF16)

    def wait_lev(part, group):
        for direction in range(2):

            @pl.when(lev_can_recv[direction])
            def _():
                lev_copy(direction, part, group).wait_recv()

    for group in range(GROUPS):
        wait_lev(0, group)
        wait_lev(2, group)

        def edges(i, _):
            slot, unit = i // units, i % units
            r = slot + 2 * (slot // 2)
            first_sweeps(group, r, unit, slot)
            return 0

        lax.fori_loop(0, 4 * units, edges, 0)
        for direction in range(2):

            @pl.when(lat_can_send[direction])
            def _():
                lat_copy(0, direction, group).start()

    for group in range(GROUPS):
        wait_lev(1, group)

        def middles(i, _):
            first_sweeps(group, 2 + i // units, i % units, None)
            return 0

        lax.fori_loop(0, 2 * units, middles, 0)

    def north_rows(state, halo, at, k, h, w_of, inv):
        def halo_row(slot):
            return halves(halo[slot, at, lane(k)].astype(F32))[h]

        base = at.start + 8 * h
        at_half = pl.ds(pl.multiple_of(base, 8), 8)
        f = [halo_row(2), halo_row(3)]
        f += [state[r, at_half, lane(k)] for r in range(rows)]
        f += [halo_row(0), halo_row(1)]
        d = [b - a for a, b in zip(f, f[1:])]
        d[1] = jnp.where(has_south, d[1], 0.0)
        d[rows + 1] = jnp.where(has_north, d[rows + 1], 0.0)
        s = [None] + [minmod(a, b) for a, b in zip(d, d[1:])]
        g = [
            face(cn[r, :, lane(k)], w_of(r, k), f[r + 1], f[r + 2], s[r + 1], s[r + 2])
            for r in range(rows + 1)
        ]
        return [f[r + 2] - inv * (g[r + 1] - g[r]) for r in range(rows)]

    def wait_lat(substep, group):
        for direction in range(2):

            @pl.when(lat_can_recv[direction])
            def _():
                lat_copy(substep, direction, group).wait_recv()

    for group in range(GROUPS):
        wait_lat(0, group)

        def middle(unit, _):
            at = pl.ds(pl.multiple_of(group * span + unit * UNIT, UNIT), UNIT)
            edge_rows = [[None, None] for _ in range(4)]
            for h in range(2):
                at_half = pl.ds(pl.multiple_of(at.start + 8 * h, 8), 8)
                inv = column_of(0, at_half)
                scale = 0.5 * inv
                swept = [
                    north_rows(
                        a_ref,
                        halo1,
                        at,
                        k,
                        h,
                        lambda r, k: hn[r, :, lane(k)] - scale * cn[r, :, lane(k)],
                        inv,
                    )
                    for k in range(chunks)
                ]
                inv = column_of(1, at_half)
                for r in range(rows):
                    c = [ce[r, :, lane(k)] for k in range(chunks)]
                    w = [we2[r, :, lane(k)] for k in range(chunks)]
                    result = east_sweep([swept[k][r] for k in range(chunks)], c, w, inv)
                    for k in range(chunks):
                        b_ref[r, at_half, lane(k)] = result[k]
                    if r < 2 or r >= rows - 2:
                        edge_rows[r if r < 2 else r - rows + 4][h] = result
            for slot in range(4):
                for k in range(chunks):
                    both = jnp.concatenate([edge_rows[slot][0][k], edge_rows[slot][1][k]], axis=0)
                    send2[slot, at, lane(k)] = both.astype(BF16)
            return 0

        lax.fori_loop(0, units, middle, 0)
        for direction in range(2):

            @pl.when(lat_can_send[direction])
            def _():
                lat_copy(1, direction, group).start()

    for group in range(GROUPS):
        wait_lat(1, group)

        def last(i, _):
            unit = i
            at = pl.ds(pl.multiple_of(group * span + unit * UNIT, UNIT), UNIT)
            for k in range(chunks):
                swept = []
                for h in range(2):
                    at_half = pl.ds(pl.multiple_of(at.start + 8 * h, 8), 8)
                    inv = column_of(1, at_half)
                    swept.append(
                        north_rows(b_ref, halo2, at, k, h, lambda r, k: wn2[r, :, lane(k)], inv)
                    )
                for r in range(rows):
                    both = jnp.concatenate([swept[0][r], swept[1][r]], axis=0)
                    h_ref[r, at, lane(k)] = both.astype(BF16)
            return 0

        lax.fori_loop(0, units, last, 0)

    def chemistry(i, _):
        r = i // chunks
        at_lane = pl.ds(pl.multiple_of(i % chunks * LANES, LANES), LANES)
        values = h_ref[r, :, at_lane]
        production = jnp.dot(rates, values, preferred_element_type=F32)
        photo = jnp.concatenate([pd[r, :, at_lane]] * (pairs // 8), axis=0)
        updated = (values.astype(F32) + photo * production) / (1.0 + photo * columns[2])
        out_ref[r, :, at_lane] = updated.astype(BF16)
        return 0

    lax.fori_loop(0, rows * chunks, chemistry, 0)

    for can_send, _, copy in wind_copies():

        @pl.when(can_send)
        def _():
            copy.wait_send()

    for group in range(GROUPS):
        for direction in range(2):

            @pl.when(lev_can_send[direction])
            def _():
                for part in range(3):
                    lev_copy(direction, part, group).wait_send()

            @pl.when(lat_can_send[direction])
            def _():
                for substep in range(2):
                    lat_copy(substep, direction, group).wait_send()


def shards(
    n_lev,
    n_lat,
    tracer_mass,
    level_wind,
    east_wind,
    north_wind,
    photolysis,
    rate_matrix,
    loss_rate,
    substeps,
    slot_table,
):
    tracers, levels, rows, lon = tracer_mass.shape
    pairs = tracers * levels

    def by_row(wind):
        return jnp.transpose(wind, (1, 0, 2))

    x = jnp.transpose(tracer_mass, (2, 0, 1, 3)).reshape(rows, pairs, lon)
    vmem = pl.BlockSpec(memory_space=pltpu.VMEM)
    field = pltpu.VMEM((rows, pairs, lon), F32)
    halo = pltpu.VMEM((4, pairs, lon), BF16)
    wide = pltpu.VMEM((rows, 8, lon), F32)
    faces = pltpu.VMEM((rows + 1, 8, lon), F32)
    half = pltpu.VMEM((rows, pairs, lon), BF16)
    dma = pltpu.SemaphoreType.DMA
    updated = pl.pallas_call(
        functools.partial(kernel, n_lev, n_lat),
        out_shape=jax.ShapeDtypeStruct((rows, pairs, lon), BF16),
        in_specs=[vmem] * 9,
        out_specs=vmem,
        scratch_shapes=[
            half,
            half,
            field,
            field,
            half,
            halo,
            halo,
            halo,
            halo,
            pltpu.VMEM((rows, levels, lon), BF16),
            wide,
            wide,
            wide,
            wide,
            wide,
            wide,
            wide,
            faces,
            faces,
            faces,
            wide,
            pltpu.VMEM((3, pairs, LANES), F32),
            dma((2, 3, GROUPS)),
            dma((2, 3, GROUPS)),
            dma((2, 2, GROUPS)),
            dma((2, 2, GROUPS)),
            dma((2,)),
            dma((2,)),
        ],
        compiler_params=pltpu.CompilerParams(
            collective_id=0, has_side_effects=True, vmem_limit_bytes=32 * 1024 * 1024
        ),
        name="transport_step",
    )(
        x,
        by_row(level_wind),
        by_row(east_wind),
        by_row(north_wind),
        by_row(photolysis),
        rate_matrix,
        loss_rate.reshape(1, tracers),
        substeps.reshape(1, tracers),
        slot_table,
    )
    return jnp.transpose(updated.reshape(rows, tracers, levels, lon), (1, 2, 0, 3))


def solution(mesh):
    return jax.shard_map(
        functools.partial(shards, mesh.shape["lev"], mesh.shape["lat"]),
        mesh=mesh,
        in_specs=(
            P(None, "lev", "lat", None),
            P("lev", "lat", None),
            P("lev", "lat", None),
            P("lev", "lat", None),
            P("lev", "lat", None),
            P(),
            P(),
            P(),
            P("lev", None),
        ),
        out_specs=P(None, "lev", "lat", None),
        check_vma=False,
    )
```

```python
import functools

import jax
import jax.numpy as jnp
from jax import lax
from jax.experimental import pallas as pl
from jax.experimental.pallas import tpu as pltpu
from jax.sharding import PartitionSpec as P

MESH = pl.DeviceIdType.MESH
CHEM_DT = 0.5
LANES = 128
GROUPS = 3
UNIT = 16

F32, BF16 = jnp.float32, jnp.bfloat16


def minmod(a, b):
    return jnp.maximum(jnp.minimum(a, b), jnp.minimum(jnp.maximum(a, b), 0.0))


def face(c, w, lower, upper, lower_slope, upper_slope):
    upwind = c > 0.0
    return c * (
        jnp.where(upwind, lower, upper) + w * jnp.where(upwind, lower_slope, upper_slope)
    )


def lane_iota():
    return lax.broadcasted_iota(jnp.int32, (8, LANES), 1)


def from_west(chunks):
    rolled = [pltpu.roll(x, 1, 1) for x in chunks]
    first = lane_iota() == 0
    return [jnp.where(first, rolled[k - 1], rolled[k]) for k in range(len(chunks))]


def from_east(chunks):
    rolled = [pltpu.roll(x, LANES - 1, 1) for x in chunks]
    last = lane_iota() == LANES - 1
    n = len(chunks)
    return [jnp.where(last, rolled[(k + 1) % n], rolled[k]) for k in range(n)]


def east_sweep(f, c, w, inv):
    fm = from_west(f)
    d = [a - b for a, b in zip(f, fm)]
    s = [minmod(a, b) for a, b in zip(from_east(d), d)]
    sm = from_west(s)
    g = [face(*args) for args in zip(c, w, fm, f, sm, s)]
    return [a - inv * (up - lo) for a, up, lo in zip(f, from_east(g), g)]


def vertical_sweep(below, own, above, c_lo, w_lo, c_hi, w_hi, even):
    m1 = jnp.where(even, pltpu.roll(below, 7, 0), pltpu.roll(own, 1, 0))
    p1 = jnp.where(even, pltpu.roll(own, 7, 0), pltpu.roll(above, 1, 0))
    d1, d2, d3, d4 = m1 - below, own - m1, p1 - own, above - p1
    sm, s0, sp = minmod(d1, d2), minmod(d2, d3), minmod(d3, d4)
    return own - (face(c_hi, w_hi, own, p1, s0, sp) - face(c_lo, w_lo, m1, own, sm, s0))


def kernel(
    n_lev,
    n_lat,
    x_ref,
    lw_ref,
    ew_ref,
    nw_ref,
    ph_ref,
    rate_ref,
    loss_ref,
    steps_ref,
    slots_ref,
    h_ref,
    keep,
    pd,
    rates_ref,
    below,
    above,
    a_ref,
    b_ref,
    send1,
    send2,
    halo1,
    halo2,
    lw_next,
    nw_next,
    cv_lo,
    wv_lo,
    cv_hi,
    wv_hi,
    ce,
    he,
    we2,
    cn,
    hn,
    wn2,
    columns,
    lev_send,
    lev_recv,
    lat_send,
    lat_recv,
    wind_send,
    wind_recv,
):
    rows, pairs, lon = h_ref.shape
    span = pairs // GROUPS
    units = span // UNIT
    chunks = lon // LANES
    lev, lat = lax.axis_index("lev"), lax.axis_index("lat")
    up, down = lax.rem(lev + 1, n_lev), lax.rem(lev + n_lev - 1, n_lev)
    north, south = lax.rem(lat + 1, n_lat), lax.rem(lat + n_lat - 1, n_lat)
    has_up, has_down = lev < n_lev - 1, lev > 0
    has_north, has_south = lat < n_lat - 1, lat > 0

    barrier = pltpu.get_barrier_semaphore()
    for to in ((up, lat), (down, lat), (lev, north), (lev, south)):
        pl.semaphore_signal(barrier, inc=1, device_id=to, device_id_type=MESH)

    def lane(k):
        return pl.ds(k * LANES, LANES)

    def remote(src, dst, send_sem, recv_sem, to):
        return pltpu.make_async_remote_copy(
            src_ref=src,
            dst_ref=dst,
            send_sem=send_sem,
            recv_sem=recv_sem,
            device_id=to,
            device_id_type=MESH,
        )

    def wind_copies():
        return (
            (has_down, has_up, remote(lw_ref, lw_next, wind_send.at[0], wind_recv.at[0], (down, lat))),
            (
                has_south,
                has_north,
                remote(nw_ref, nw_next, wind_send.at[1], wind_recv.at[1], (lev, south)),
            ),
        )

    def lev_copy(direction, part, group):
        to = ((up, lat), (down, lat))[direction]
        where = pl.ds(2 * part, 2), pl.ds(group * span, span)
        return remote(
            x_ref.at[where],
            (below, above)[direction].at[where],
            lev_send.at[direction, part, group],
            lev_recv.at[direction, part, group],
            to,
        )

    def lat_copy(substep, direction, group):
        to = ((lev, south), (lev, north))[direction]
        where = pl.ds(2 * direction, 2), pl.ds(group * span, span)
        return remote(
            (send1, send2)[substep].at[where],
            (halo1, halo2)[substep].at[where],
            lat_send.at[substep, direction, group],
            lat_recv.at[substep, direction, group],
            to,
        )

    lev_can_send, lev_can_recv = (has_up, has_down), (has_down, has_up)
    lat_can_send, lat_can_recv = (has_south, has_north), (has_north, has_south)

    pl.semaphore_wait(barrier, 4)
    for can_send, _, copy in wind_copies():

        @pl.when(can_send)
        def _():
            copy.start()

    for part, group in [(p, g) for g in range(GROUPS) for p in (0, 2)] + [(1, g) for g in range(GROUPS)]:
        for direction in range(2):

            @pl.when(lev_can_send[direction])
            def _():
                lev_copy(direction, part, group).start()

    even = lax.broadcasted_iota(jnp.int32, (8, LANES), 0) % 2 == 0

    def pattern(ref, r):
        v = ref[r].astype(F32)
        return jnp.concatenate([v] * 4, axis=0)

    even_row = lax.broadcasted_iota(jnp.int32, (8, lon), 0) % 2 == 0

    def tables(r, _):
        c = pattern(nw_ref, r)
        c = jnp.where((r == 0) & ~has_south, 0.0, c)
        cn[r] = c
        c = pattern(ew_ref, r)
        half = jnp.where(c > 0.0, 0.5, -0.5)
        ce[r] = c
        he[r] = half
        we2[r] = half - 0.25 * c
        c = pattern(lw_ref, r)
        c = jnp.where(even_row & ~has_down, 0.0, c)
        cv_lo[r] = c
        wv_lo[r] = jnp.where(c > 0.0, 0.5, -0.5) - 0.5 * c
        pd[r] = CHEM_DT * pattern(ph_ref, r)
        return 0

    lax.fori_loop(0, rows, tables, 0)

    pair_of = lax.broadcasted_iota(jnp.int32, (pairs, pairs // 2), 0) // 2
    tracer_of = lax.broadcasted_iota(jnp.int32, (pairs, pairs // 2), 1)
    picks = pair_of == tracer_of

    def column(row):
        value = jnp.sum(jnp.where(picks, row, 0.0), axis=1, keepdims=True)
        return jnp.broadcast_to(value, (pairs, LANES))

    steps = steps_ref[...]
    carried = slots_ref[...] >= 0
    first = jnp.where(carried, jnp.where(steps > 1, 0.5, 1.0), 0.0)
    second = jnp.where(carried & (steps > 1), 0.5, 0.0)
    columns[0] = column(first)
    columns[1] = column(second)
    columns[2] = column(loss_ref[...])
    expand = picks.astype(BF16)
    spread = lax.dot_general(
        expand, rate_ref[...], (((1,), (1,)), ((), ())), preferred_element_type=F32
    ).astype(BF16)
    spread = lax.dot_general(
        spread, expand, (((1,), (1,)), ((), ())), preferred_element_type=F32
    )
    same = (
        lax.broadcasted_iota(jnp.int32, (pairs, pairs), 0) % 2
        == lax.broadcasted_iota(jnp.int32, (pairs, pairs), 1) % 2
    )
    rates_ref[...] = jnp.where(same, spread, 0.0).astype(BF16)

    def all_units(body):
        lax.fori_loop(0, rows * (pairs // UNIT), body, 0)

    def halves(value):
        return value[:8], value[8:]

    @pl.when(~has_down)
    def _():
        def fill(i, _):
            r, at = i // (pairs // UNIT), pl.ds(pl.multiple_of(i % (pairs // UNIT) * UNIT, UNIT), UNIT)
            for k in range(chunks):
                here = r, at, lane(k)
                parts = [
                    jnp.where(even, v, pltpu.roll(v, 1, 0)) for v in halves(x_ref[here].astype(F32))
                ]
                below[here] = jnp.concatenate(parts, axis=0).astype(BF16)
            return 0

        all_units(fill)

    @pl.when(~has_up)
    def _():
        def fill(i, _):
            r, at = i // (pairs // UNIT), pl.ds(pl.multiple_of(i % (pairs // UNIT) * UNIT, UNIT), UNIT)
            for k in range(chunks):
                here = r, at, lane(k)
                parts = [
                    jnp.where(even, pltpu.roll(v, 7, 0), v) for v in halves(x_ref[here].astype(F32))
                ]
                above[here] = jnp.concatenate(parts, axis=0).astype(BF16)
            return 0

        all_units(fill)
        lw_next[...] = jnp.zeros(lw_next.shape, BF16)

    for at_edge, where in ((~has_north, 0), (~has_south, 2)):

        @pl.when(at_edge)
        def _():
            zero = jnp.zeros((2, pairs, lon), BF16)
            halo1[pl.ds(where, 2)] = zero
            halo2[pl.ds(where, 2)] = zero

    @pl.when(~has_north)
    def _():
        nw_next[...] = jnp.zeros(nw_next.shape, BF16)

    def loss_table(r, _):
        photo = jnp.concatenate([pd[r]] * (pairs // 8), axis=0)
        for k in range(chunks):
            part = pl.ds(k * LANES, LANES)
            keep[r, :, part] = 1.0 / (1.0 + photo[:, k * LANES : (k + 1) * LANES] * columns[2])
        return 0

    lax.fori_loop(0, rows, loss_table, 0)

    for _, can_recv, copy in wind_copies():

        @pl.when(can_recv)
        def _():
            copy.wait_recv()

    def more_tables(r, _):
        mine, theirs = pattern(lw_ref, r), pattern(lw_next, r)
        c = jnp.where(even_row, pltpu.roll(mine, 7, 0), pltpu.roll(theirs, 1, 0))
        c = jnp.where(~even_row & ~has_up, 0.0, c)
        cv_hi[r] = c
        wv_hi[r] = jnp.where(c > 0.0, 0.5, -0.5) - 0.5 * c
        return 0

    lax.fori_loop(0, rows, more_tables, 0)

    cn[rows] = pattern(nw_next, 0)

    def north_tables(r, _):
        c = cn[r]
        half = jnp.where(c > 0.0, 0.5, -0.5)
        hn[r] = half
        wn2[r] = half - 0.25 * c
        return 0

    lax.fori_loop(0, rows + 1, north_tables, 0)

    def column_of(which, at):
        return columns[which, at, :]

    def first_sweeps(group, r, unit, slot):
        base = pl.multiple_of(group * span + unit * UNIT, UNIT)
        at = pl.ds(base, UNIT)
        swept = []
        for k in range(chunks):
            here = r, at, lane(k)
            lo, own, hi = (halves(ref[here].astype(F32)) for ref in (below, x_ref, above))
            tables_here = [ref[r, :, lane(k)] for ref in (cv_lo, wv_lo, cv_hi, wv_hi)]
            moved = [vertical_sweep(lo[h], own[h], hi[h], *tables_here, even) for h in range(2)]
            swept.append(jnp.concatenate(moved, axis=0).astype(BF16).astype(F32))
        c = [ce[r, :, lane(k)] for k in range(chunks)]
        half = [he[r, :, lane(k)] for k in range(chunks)]
        after = []
        for h in range(2):
            at_half = pl.ds(pl.multiple_of(base + 8 * h, 8), 8)
            inv = column_of(0, at_half)
            scale = 0.5 * inv
            w = [b - scale * a for a, b in zip(c, half)]
            result = east_sweep([halves(v)[h] for v in swept], c, w, inv)
            for k in range(chunks):
                a_ref[r, at_half, lane(k)] = result[k]
            after.append(result)
        if slot is not None:
            for k in range(chunks):
                both = jnp.concatenate([after[0][k], after[1][k]], axis=0)
                send1[slot, at, lane(k)] = both.astype(BF16)

    def wait_lev(part, group):
        for direction in range(2):

            @pl.when(lev_can_recv[direction])
            def _():
                lev_copy(direction, part, group).wait_recv()

    for group in range(GROUPS):
        wait_lev(0, group)
        wait_lev(2, group)

        def edges(unit, _):
            for slot, r in enumerate((0, 1, rows - 2, rows - 1)):
                first_sweeps(group, r, unit, slot)
            return 0

        lax.fori_loop(0, units, edges, 0)
        for direction in range(2):

            @pl.when(lat_can_send[direction])
            def _():
                lat_copy(0, direction, group).start()

    def middles(group):
        wait_lev(1, group)
        for unit in range(units):
            for r in range(2, rows - 2):
                first_sweeps(group, r, unit, None)

    def north_rows(state, halo, at, k, h, w_of, inv):
        def halo_row(slot):
            return halves(halo[slot, at, lane(k)].astype(F32))[h]

        base = at.start + 8 * h
        at_half = pl.ds(pl.multiple_of(base, 8), 8)
        f = [halo_row(2), halo_row(3)]
        f += [state[r, at_half, lane(k)] for r in range(rows)]
        f += [halo_row(0), halo_row(1)]
        d = [b - a for a, b in zip(f, f[1:])]
        d[1] = jnp.where(has_south, d[1], 0.0)
        d[rows + 1] = jnp.where(has_north, d[rows + 1], 0.0)
        s = [None] + [minmod(a, b) for a, b in zip(d, d[1:])]
        g = [
            face(cn[r, :, lane(k)], w_of(r, k), f[r + 1], f[r + 2], s[r + 1], s[r + 2])
            for r in range(rows + 1)
        ]
        return [f[r + 2] - inv * (g[r + 1] - g[r]) for r in range(rows)]

    def wait_lat(substep, group):
        for direction in range(2):

            @pl.when(lat_can_recv[direction])
            def _():
                lat_copy(substep, direction, group).wait_recv()

    for group in range(GROUPS):
        middles(group)
        wait_lat(0, group)

        def middle(unit, _):
            at = pl.ds(pl.multiple_of(group * span + unit * UNIT, UNIT), UNIT)
            edge_rows = [[None, None] for _ in range(4)]
            for h in range(2):
                at_half = pl.ds(pl.multiple_of(at.start + 8 * h, 8), 8)
                inv = column_of(0, at_half)
                scale = 0.5 * inv
                swept = [
                    north_rows(
                        a_ref,
                        halo1,
                        at,
                        k,
                        h,
                        lambda r, k: hn[r, :, lane(k)] - scale * cn[r, :, lane(k)],
                        inv,
                    )
                    for k in range(chunks)
                ]
                inv = column_of(1, at_half)
                for r in range(rows):
                    c = [ce[r, :, lane(k)] for k in range(chunks)]
                    w = [we2[r, :, lane(k)] for k in range(chunks)]
                    result = east_sweep([swept[k][r] for k in range(chunks)], c, w, inv)
                    for k in range(chunks):
                        b_ref[r, at_half, lane(k)] = result[k]
                    if r < 2 or r >= rows - 2:
                        edge_rows[r if r < 2 else r - rows + 4][h] = result
            for slot in range(4):
                for k in range(chunks):
                    both = jnp.concatenate([edge_rows[slot][0][k], edge_rows[slot][1][k]], axis=0)
                    send2[slot, at, lane(k)] = both.astype(BF16)
            return 0

        lax.fori_loop(0, units, middle, 0)
        for direction in range(2):

            @pl.when(lat_can_send[direction])
            def _():
                lat_copy(1, direction, group).start()

    for group in range(GROUPS):
        wait_lat(1, group)

        def last(i, _):
            unit = i
            at = pl.ds(pl.multiple_of(group * span + unit * UNIT, UNIT), UNIT)
            for k in range(chunks):
                swept = []
                for h in range(2):
                    at_half = pl.ds(pl.multiple_of(at.start + 8 * h, 8), 8)
                    inv = column_of(1, at_half)
                    swept.append(
                        north_rows(b_ref, halo2, at, k, h, lambda r, k: wn2[r, :, lane(k)], inv)
                    )
                for r in range(rows):
                    both = jnp.concatenate([swept[0][r], swept[1][r]], axis=0)
                    h_ref[r, at, lane(k)] = both.astype(BF16)
            return 0

        lax.fori_loop(0, units, last, 0)

    for can_send, _, copy in wind_copies():

        @pl.when(can_send)
        def _():
            copy.wait_send()

    for group in range(GROUPS):
        for direction in range(2):

            @pl.when(lev_can_send[direction])
            def _():
                for part in range(3):
                    lev_copy(direction, part, group).wait_send()

            @pl.when(lat_can_send[direction])
            def _():
                for substep in range(2):
                    lat_copy(substep, direction, group).wait_send()


def chemistry(h_ref, keep, pd, rates_ref, out_ref, y_ref, out_sem):
    rows, pairs, lon = h_ref.shape
    chunks = lon // LANES
    copies = []
    for r in range(rows):
        values = h_ref[r]
        production = jnp.dot(rates_ref[...], values, preferred_element_type=F32)
        photo = jnp.concatenate([pd[r]] * (pairs // 8), axis=0)
        updated = ((values.astype(F32) + photo * production) * keep[r]).astype(BF16)
        for k in range(chunks):
            part = pl.ds(k * LANES, LANES)
            y_ref.reshape(rows, chunks, pairs, LANES)[r, k] = updated[:, k * LANES : (k + 1) * LANES]
            copy = pltpu.make_async_copy(y_ref.at[r, k], out_ref.at[:, r, :, part], out_sem.at[r, k])
            copy.start()
            copies.append(copy)
    for copy in copies:
        copy.wait()


def shards(
    n_lev,
    n_lat,
    tracer_mass,
    level_wind,
    east_wind,
    north_wind,
    photolysis,
    rate_matrix,
    loss_rate,
    substeps,
    slot_table,
):
    tracers, levels, rows, lon = tracer_mass.shape
    pairs = tracers * levels

    def by_row(wind):
        return jnp.transpose(wind, (1, 0, 2))

    vmem = pl.BlockSpec(memory_space=pltpu.VMEM)
    hbm = pl.BlockSpec(memory_space=pltpu.HBM)
    field = pltpu.VMEM((rows, pairs, lon), F32)
    halo = pltpu.VMEM((4, pairs, lon), BF16)
    wide = pltpu.VMEM((rows, 8, lon), F32)
    faces = pltpu.VMEM((rows + 1, 8, lon), F32)
    half = pltpu.VMEM((rows, pairs, lon), BF16)
    tiles = pltpu.VMEM((rows, lon // LANES, tracers, levels, LANES), BF16)
    dma = pltpu.SemaphoreType.DMA
    moved, keep, photo, rates = pl.pallas_call(
        functools.partial(kernel, n_lev, n_lat),
        out_shape=[
            jax.ShapeDtypeStruct((rows, pairs, lon), BF16),
            jax.ShapeDtypeStruct((rows, pairs, lon), F32),
            jax.ShapeDtypeStruct((rows, 8, lon), F32),
            jax.ShapeDtypeStruct((pairs, pairs), BF16),
        ],
        in_specs=[vmem] * 9,
        out_specs=[vmem] * 4,
        scratch_shapes=[
            half,
            half,
            field,
            field,
            halo,
            halo,
            halo,
            halo,
            pltpu.VMEM((rows, levels, lon), BF16),
            pltpu.VMEM((rows, levels, lon), BF16),
            wide,
            wide,
            wide,
            wide,
            wide,
            wide,
            wide,
            faces,
            faces,
            faces,
            pltpu.VMEM((3, pairs, LANES), F32),
            dma((2, 3, GROUPS)),
            dma((2, 3, GROUPS)),
            dma((2, 2, GROUPS)),
            dma((2, 2, GROUPS)),
            dma((2,)),
            dma((2,)),
        ],
        compiler_params=pltpu.CompilerParams(
            collective_id=0, has_side_effects=True, vmem_limit_bytes=32 * 1024 * 1024
        ),
        name="transport",
    )(
        jnp.transpose(tracer_mass, (2, 0, 1, 3)).reshape(rows, pairs, lon),
        by_row(level_wind),
        by_row(east_wind),
        by_row(north_wind),
        by_row(photolysis),
        rate_matrix,
        loss_rate.reshape(1, tracers),
        substeps.reshape(1, tracers),
        slot_table,
    )
    updated = pl.pallas_call(
        chemistry,
        out_shape=jax.ShapeDtypeStruct((tracers, rows, levels, lon), BF16),
        in_specs=[vmem] * 4,
        out_specs=hbm,
        scratch_shapes=[tiles, dma((rows, lon // LANES))],
        compiler_params=pltpu.CompilerParams(vmem_limit_bytes=16 * 1024 * 1024),
        name="chemistry",
    )(moved, keep, photo, rates)
    return jnp.transpose(updated, (0, 2, 1, 3))


def solution(mesh):
    return jax.shard_map(
        functools.partial(shards, mesh.shape["lev"], mesh.shape["lat"]),
        mesh=mesh,
        in_specs=(
            P(None, "lev", "lat", None),
            P("lev", "lat", None),
            P("lev", "lat", None),
            P("lev", "lat", None),
            P("lev", "lat", None),
            P(),
            P(),
            P(),
            P("lev", None),
        ),
        out_specs=P(None, "lev", "lat", None),
        check_vma=False,
    )
```

```python
import functools

import jax
import jax.numpy as jnp
from jax import lax
from jax.experimental import pallas as pl
from jax.experimental.pallas import tpu as pltpu
from jax.sharding import PartitionSpec as P

MESH = pl.DeviceIdType.MESH
CHEM_DT = 0.5
LANES = 128
GROUPS = 6
LAG = 3
REACH = 4
UNIT = 16

F32, BF16 = jnp.float32, jnp.bfloat16


def minmod(a, b):
    zero = jnp.zeros((), a.dtype)
    return jnp.maximum(jnp.minimum(a, b), jnp.minimum(jnp.maximum(a, b), zero))


def face(c, w, lower, upper, lower_slope, upper_slope):
    slope = w * jnp.where(w > 0, lower_slope, upper_slope)
    return c * (jnp.where(c > 0.0, lower, upper) + slope.astype(F32))


def lane_iota():
    return lax.broadcasted_iota(jnp.int32, (UNIT, LANES), 1)


def from_west(chunks):
    rolled = [pltpu.roll(x, 1, 1) for x in chunks]
    first = lane_iota() == 0
    return [jnp.where(first, rolled[k - 1], rolled[k]) for k in range(len(chunks))]


def from_east(chunks):
    rolled = [pltpu.roll(x, LANES - 1, 1) for x in chunks]
    last = lane_iota() == LANES - 1
    n = len(chunks)
    return [jnp.where(last, rolled[(k + 1) % n], rolled[k]) for k in range(n)]


def east_sweep(f, c, w, inv):
    fm = from_west(f)
    d = [a.astype(BF16) - b.astype(BF16) for a, b in zip(f, fm)]
    s = [minmod(a, b) for a, b in zip(from_east(d), d)]
    sm = from_west(s)
    g = [face(*args) for args in zip(c, w, fm, f, sm, s)]
    return [a - inv * (up - lo) for a, up, lo in zip(f, from_east(g), g)]


def roll_pairs(x, shift):
    return jnp.concatenate([pltpu.roll(x[:8], shift, 0), pltpu.roll(x[8:], shift, 0)], axis=0)


def vertical_sweep(below, own, above, c_lo, w_lo, c_hi, w_hi, even):
    f = own.astype(F32)
    m1 = jnp.where(even, roll_pairs(below.astype(F32), 7), roll_pairs(f, 1))
    p1 = jnp.where(even, roll_pairs(f, 7), roll_pairs(above.astype(F32), 1))
    m1b, p1b = m1.astype(BF16), p1.astype(BF16)
    d1, d2, d3, d4 = m1b - below, own - m1b, p1b - own, above - p1b
    sm, s0, sp = minmod(d1, d2), minmod(d2, d3), minmod(d3, d4)
    return f - (face(c_hi, w_hi, f, p1, s0, sp) - face(c_lo, w_lo, m1, f, sm, s0))


def kernel(
    n_lev,
    n_lat,
    x_ref,
    lw_ref,
    ew_ref,
    nw_ref,
    ph_ref,
    rate_ref,
    loss_ref,
    steps_ref,
    slots_ref,
    h_ref,
    keep,
    pd,
    rates_ref,
    below,
    above,
    a_ref,
    send,
    halo,
    lw_next,
    ew_south,
    ew_north,
    nw_south,
    nw_north,
    cv_lo,
    wv_lo,
    cv_hi,
    wv_hi,
    ce,
    be,
    he,
    we2,
    cn,
    bn,
    hn,
    wn2,
    columns,
    lev_send,
    lev_recv,
    lat_send,
    lat_recv,
    wind_send,
    wind_recv,
):
    rows, pairs, lon = h_ref.shape
    span = pairs // GROUPS
    units = span // UNIT
    chunks = lon // LANES
    lev, lat = lax.axis_index("lev"), lax.axis_index("lat")
    up, down = lax.rem(lev + 1, n_lev), lax.rem(lev + n_lev - 1, n_lev)
    north, south = lax.rem(lat + 1, n_lat), lax.rem(lat + n_lat - 1, n_lat)
    has_up, has_down = lev < n_lev - 1, lev > 0
    has_north, has_south = lat < n_lat - 1, lat > 0

    barrier = pltpu.get_barrier_semaphore()
    for to in ((up, lat), (down, lat), (lev, north), (lev, south)):
        pl.semaphore_signal(barrier, inc=1, device_id=to, device_id_type=MESH)

    def lane(k):
        return pl.ds(k * LANES, LANES)

    def remote(src, dst, send_sem, recv_sem, to):
        return pltpu.make_async_remote_copy(
            src_ref=src,
            dst_ref=dst,
            send_sem=send_sem,
            recv_sem=recv_sem,
            device_id=to,
            device_id_type=MESH,
        )

    def wind_copies():
        def wind(n, can_send, can_recv, src, dst, to):
            return can_send, can_recv, remote(src, dst, wind_send.at[n], wind_recv.at[n], to)

        return (
            wind(0, has_down, has_up, lw_ref, lw_next, (down, lat)),
            wind(1, has_south, has_north, ew_ref, ew_north, (lev, south)),
            wind(2, has_north, has_south, ew_ref, ew_south, (lev, north)),
            wind(3, has_south, has_north, nw_ref, nw_north, (lev, south)),
            wind(4, has_north, has_south, nw_ref, nw_south, (lev, north)),
        )

    def members(group):
        return pl.ds(group * span, span)

    def lev_copy(direction, group):
        to = ((up, lat), (down, lat))[direction]
        where = pl.ds(0, rows), members(group)
        return remote(
            x_ref.at[where],
            (below, above)[direction].at[where],
            lev_send.at[direction, group],
            lev_recv.at[direction, group],
            to,
        )

    def lat_copy(direction, group):
        to = ((lev, south), (lev, north))[direction]
        first_row = (0, rows - REACH)[direction]
        return remote(
            send.at[pl.ds(first_row, REACH), members(group)],
            halo.at[pl.ds(REACH * direction, REACH), members(group)],
            lat_send.at[direction, group],
            lat_recv.at[direction, group],
            to,
        )

    lev_can_send, lev_can_recv = (has_up, has_down), (has_down, has_up)
    lat_can_send, lat_can_recv = (has_south, has_north), (has_north, has_south)

    pl.semaphore_wait(barrier, 4)
    for group in range(GROUPS):
        for direction in range(2):

            @pl.when(lev_can_send[direction])
            def _():
                lev_copy(direction, group).start()

        if group == 0:
            for can_send, _, copy in wind_copies():

                @pl.when(can_send)
                def _():
                    copy.start()

    even8 = lax.broadcasted_iota(jnp.int32, (8, LANES), 0) % 2 == 0
    even = lax.broadcasted_iota(jnp.int32, (UNIT, LANES), 0) % 2 == 0

    def pattern(ref, r):
        v = ref[r].astype(F32)
        return jnp.concatenate([v] * 4, axis=0)

    even_row = lax.broadcasted_iota(jnp.int32, (8, lon), 0) % 2 == 0

    def doubled(value):
        return jnp.concatenate([value, value], axis=0).astype(BF16)

    def north_tables(face, c):
        half = jnp.where(c > 0.0, 0.5, -0.5)
        cn[face] = c
        bn[face] = doubled(c)
        hn[face] = doubled(half)
        wn2[face] = doubled(half - 0.25 * c)

    def east_tables(row, c):
        half = jnp.where(c > 0.0, 0.5, -0.5)
        ce[row] = c
        be[row] = doubled(c)
        he[row] = doubled(half)
        we2[row] = doubled(half - 0.25 * c)

    def tables(r, _):
        c = pattern(nw_ref, r)
        north_tables(r + 2, jnp.where((r == 0) & ~has_south, 0.0, c))
        east_tables(r + 2, pattern(ew_ref, r))
        c = pattern(lw_ref, r)
        c = jnp.where(even_row & ~has_down, 0.0, c)
        cv_lo[r] = c
        wv_lo[r] = doubled(jnp.where(c > 0.0, 0.5, -0.5) - 0.5 * c)
        pd[r] = CHEM_DT * pattern(ph_ref, r)
        return 0

    lax.fori_loop(0, rows, tables, 0)

    pair_of = lax.broadcasted_iota(jnp.int32, (pairs, pairs // 2), 0) // 2
    tracer_of = lax.broadcasted_iota(jnp.int32, (pairs, pairs // 2), 1)
    picks = pair_of == tracer_of

    def column(row):
        value = jnp.sum(jnp.where(picks, row, 0.0), axis=1, keepdims=True)
        return jnp.broadcast_to(value, (pairs, LANES))

    steps = steps_ref[...]
    carried = slots_ref[...] >= 0
    first = jnp.where(carried, jnp.where(steps > 1, 0.5, 1.0), 0.0)
    second = jnp.where(carried & (steps > 1), 0.5, 0.0)
    columns[0] = column(first)
    columns[1] = column(second)
    columns[2] = column(loss_ref[...])
    expand = picks.astype(BF16)
    spread = lax.dot_general(
        expand, rate_ref[...], (((1,), (1,)), ((), ())), preferred_element_type=F32
    ).astype(BF16)
    spread = lax.dot_general(
        spread, expand, (((1,), (1,)), ((), ())), preferred_element_type=F32
    )
    same = (
        lax.broadcasted_iota(jnp.int32, (pairs, pairs), 0) % 2
        == lax.broadcasted_iota(jnp.int32, (pairs, pairs), 1) % 2
    )
    rates_ref[...] = jnp.where(same, spread, 0.0).astype(BF16)

    def all_units(body):
        lax.fori_loop(0, rows * (pairs // UNIT), body, 0)

    def halves(value):
        return value[:8], value[8:]

    @pl.when(~has_down)
    def _():
        def fill(i, _):
            r, at = i // (pairs // UNIT), pl.ds(pl.multiple_of(i % (pairs // UNIT) * UNIT, UNIT), UNIT)
            for k in range(chunks):
                here = r, at, lane(k)
                parts = [
                    jnp.where(even8, v, pltpu.roll(v, 1, 0)) for v in halves(x_ref[here].astype(F32))
                ]
                below[here] = jnp.concatenate(parts, axis=0).astype(BF16)
            return 0

        all_units(fill)

    @pl.when(~has_up)
    def _():
        def fill(i, _):
            r, at = i // (pairs // UNIT), pl.ds(pl.multiple_of(i % (pairs // UNIT) * UNIT, UNIT), UNIT)
            for k in range(chunks):
                here = r, at, lane(k)
                parts = [
                    jnp.where(even8, pltpu.roll(v, 7, 0), v) for v in halves(x_ref[here].astype(F32))
                ]
                above[here] = jnp.concatenate(parts, axis=0).astype(BF16)
            return 0

        all_units(fill)
        lw_next[...] = jnp.zeros(lw_next.shape, BF16)

    for at_edge, where, wind in ((~has_north, 0, (ew_north, nw_north)), (~has_south, REACH, (ew_south, nw_south))):

        @pl.when(at_edge)
        def _():
            halo[pl.ds(where, REACH)] = jnp.zeros((REACH, pairs, lon), BF16)
            for ref in wind:
                ref[...] = jnp.zeros(ref.shape, BF16)

    def loss_table(r, _):
        photo = jnp.concatenate([pd[r]] * (pairs // 8), axis=0)
        for k in range(chunks):
            part = pl.ds(k * LANES, LANES)
            keep[r, :, part] = 1.0 / (1.0 + photo[:, k * LANES : (k + 1) * LANES] * columns[2])
        return 0

    lax.fori_loop(0, rows, loss_table, 0)

    for _, can_recv, copy in wind_copies():

        @pl.when(can_recv)
        def _():
            copy.wait_recv()

    def more_tables(r, _):
        mine, theirs = pattern(lw_ref, r), pattern(lw_next, r)
        c = jnp.where(even_row, pltpu.roll(mine, 7, 0), pltpu.roll(theirs, 1, 0))
        c = jnp.where(~even_row & ~has_up, 0.0, c)
        cv_hi[r] = c
        wv_hi[r] = doubled(jnp.where(c > 0.0, 0.5, -0.5) - 0.5 * c)
        return 0

    lax.fori_loop(0, rows, more_tables, 0)

    for r in range(2):
        east_tables(r, pattern(ew_south, rows - 2 + r))
        east_tables(rows + 2 + r, pattern(ew_north, r))
        north_tables(r, pattern(nw_south, rows - 2 + r))
    for r in range(3):
        north_tables(rows + 2 + r, pattern(nw_north, r))

    def column_of(which, at):
        return columns[which, at, :]

    def both(ref, i, k):
        value = ref[i, :, lane(k)]
        return jnp.concatenate([value, value], axis=0)

    def first_sweeps(group, r, unit):
        at = pl.ds(group * span + unit * UNIT, UNIT)
        swept = []
        for k in range(chunks):
            here = r, at, lane(k)
            moved = vertical_sweep(
                below[here],
                x_ref[here],
                above[here],
                both(cv_lo, r, k),
                wv_lo[r, :, lane(k)],
                both(cv_hi, r, k),
                wv_hi[r, :, lane(k)],
                even,
            )
            swept.append(moved.astype(BF16).astype(F32))
        inv = column_of(0, at)
        scale = (0.5 * inv).astype(BF16)
        c = [both(ce, r + 2, k) for k in range(chunks)]
        w = [he[r + 2, :, lane(k)] - scale * be[r + 2, :, lane(k)] for k in range(chunks)]
        result = east_sweep(swept, c, w, inv)
        for k in range(chunks):
            a_ref[r, at, lane(k)] = result[k]
            send[r, at, lane(k)] = result[k].astype(BF16)

    def early(group):
        for direction in range(2):

            @pl.when(lev_can_recv[direction])
            def _():
                lev_copy(direction, group).wait_recv()

        for unit in range(units):
            for r in range(rows):
                first_sweeps(group, r, unit)
        for direction in range(2):

            @pl.when(lat_can_send[direction])
            def _():
                lat_copy(direction, group).start()

    def north_sweep(f, first_face, k, w_of, inv):
        count = len(f) - 4
        b = [v.astype(BF16) for v in f]
        d = [hi - lo for lo, hi in zip(b, b[1:])]
        south_edge, north_edge = 2 - first_face + 1, rows + 2 - first_face + 1
        zero = jnp.zeros((UNIT, LANES), BF16)
        d[south_edge] = jnp.where(has_south, d[south_edge], zero)
        d[north_edge] = jnp.where(has_north, d[north_edge], zero)
        s = [None] + [minmod(lo, hi) for lo, hi in zip(d, d[1:])]
        g = [
            face(both(cn, first_face + i, k), w_of(first_face + i, k), f[i + 1], f[i + 2], s[i + 1], s[i + 2])
            for i in range(count + 1)
        ]
        return [f[i + 2] - inv * (g[i + 1] - g[i]) for i in range(count)]

    def late_sweeps(group, unit):
        at = pl.ds(group * span + unit * UNIT, UNIT)
        inv = column_of(0, at)
        scale = (0.5 * inv).astype(BF16)
        swept = []
        for k in range(chunks):
            f = [halo[REACH + i, at, lane(k)].astype(F32) for i in range(REACH)]
            f += [a_ref[r, at, lane(k)] for r in range(rows)]
            f += [halo[i, at, lane(k)].astype(F32) for i in range(REACH)]
            swept.append(
                north_sweep(f, 0, k, lambda i, k: hn[i, :, lane(k)] - scale * bn[i, :, lane(k)], inv)
            )
        inv = column_of(1, at)
        for r in range(rows + 4):
            c = [both(ce, r, k) for k in range(chunks)]
            w = [we2[r, :, lane(k)] for k in range(chunks)]
            row = east_sweep([swept[k][r] for k in range(chunks)], c, w, inv)
            for k in range(chunks):
                swept[k][r] = row[k]
        for k in range(chunks):
            result = north_sweep(swept[k], 2, k, lambda i, k: wn2[i, :, lane(k)], inv)
            for r in range(rows):
                h_ref[r, at, lane(k)] = result[r].astype(BF16)

    def late(group):
        for direction in range(2):

            @pl.when(lat_can_recv[direction])
            def _():
                lat_copy(direction, group).wait_recv()

        for unit in range(units):
            late_sweeps(group, unit)

    for step in range(GROUPS + LAG):
        if step < GROUPS:
            early(step)
        if step >= LAG:
            late(step - LAG)

    for can_send, _, copy in wind_copies():

        @pl.when(can_send)
        def _():
            copy.wait_send()

    for group in range(GROUPS):
        for direction in range(2):

            @pl.when(lev_can_send[direction])
            def _():
                lev_copy(direction, group).wait_send()

            @pl.when(lat_can_send[direction])
            def _():
                lat_copy(direction, group).wait_send()


def chemistry(h_ref, keep, pd, rates_ref, out_ref, y_ref, out_sem):
    rows, pairs, lon = h_ref.shape
    chunks = lon // LANES
    copies = []
    for r in range(rows):
        values = h_ref[r]
        production = jnp.dot(rates_ref[...], values, preferred_element_type=F32)
        photo = jnp.concatenate([pd[r]] * (pairs // 8), axis=0)
        updated = ((values.astype(F32) + photo * production) * keep[r]).astype(BF16)
        for k in range(chunks):
            part = pl.ds(k * LANES, LANES)
            y_ref.reshape(rows, chunks, pairs, LANES)[r, k] = updated[:, k * LANES : (k + 1) * LANES]
            copy = pltpu.make_async_copy(y_ref.at[r, k], out_ref.at[:, r, :, part], out_sem.at[r, k])
            copy.start()
            copies.append(copy)
    for copy in copies:
        copy.wait()


def shards(
    n_lev,
    n_lat,
    tracer_mass,
    level_wind,
    east_wind,
    north_wind,
    photolysis,
    rate_matrix,
    loss_rate,
    substeps,
    slot_table,
):
    tracers, levels, rows, lon = tracer_mass.shape
    pairs = tracers * levels

    def by_row(wind):
        return jnp.transpose(wind, (1, 0, 2))

    vmem = pl.BlockSpec(memory_space=pltpu.VMEM)
    hbm = pl.BlockSpec(memory_space=pltpu.HBM)
    field = pltpu.VMEM((rows, pairs, lon), F32)
    wind = pltpu.VMEM((rows, levels, lon), BF16)

    def wide(count):
        return pltpu.VMEM((count, 8, lon), F32)

    def twice(count):
        return pltpu.VMEM((count, UNIT, lon), BF16)

    half = pltpu.VMEM((rows, pairs, lon), BF16)
    tiles = pltpu.VMEM((rows, lon // LANES, tracers, levels, LANES), BF16)
    dma = pltpu.SemaphoreType.DMA
    moved, keep, photo, rates = pl.pallas_call(
        functools.partial(kernel, n_lev, n_lat),
        out_shape=[
            jax.ShapeDtypeStruct((rows, pairs, lon), BF16),
            jax.ShapeDtypeStruct((rows, pairs, lon), F32),
            jax.ShapeDtypeStruct((rows, 8, lon), F32),
            jax.ShapeDtypeStruct((pairs, pairs), BF16),
        ],
        in_specs=[vmem] * 9,
        out_specs=[vmem] * 4,
        scratch_shapes=[
            half,
            half,
            field,
            half,
            pltpu.VMEM((2 * REACH, pairs, lon), BF16),
            wind,
            wind,
            wind,
            wind,
            wind,
            wide(rows),
            twice(rows),
            wide(rows),
            twice(rows),
            wide(rows + 4),
            twice(rows + 4),
            twice(rows + 4),
            twice(rows + 4),
            wide(rows + 5),
            twice(rows + 5),
            twice(rows + 5),
            twice(rows + 5),
            pltpu.VMEM((3, pairs, LANES), F32),
            dma((2, GROUPS)),
            dma((2, GROUPS)),
            dma((2, GROUPS)),
            dma((2, GROUPS)),
            dma((5,)),
            dma((5,)),
        ],
        compiler_params=pltpu.CompilerParams(
            collective_id=0, has_side_effects=True, vmem_limit_bytes=32 * 1024 * 1024
        ),
        name="transport",
    )(
        jnp.transpose(tracer_mass, (2, 0, 1, 3)).reshape(rows, pairs, lon),
        by_row(level_wind),
        by_row(east_wind),
        by_row(north_wind),
        by_row(photolysis),
        rate_matrix,
        loss_rate.reshape(1, tracers),
        substeps.reshape(1, tracers),
        slot_table,
    )
    updated = pl.pallas_call(
        chemistry,
        out_shape=jax.ShapeDtypeStruct((tracers, rows, levels, lon), BF16),
        in_specs=[vmem] * 4,
        out_specs=hbm,
        scratch_shapes=[tiles, dma((rows, lon // LANES))],
        compiler_params=pltpu.CompilerParams(vmem_limit_bytes=16 * 1024 * 1024),
        name="chemistry",
    )(moved, keep, photo, rates)
    return jnp.transpose(updated, (0, 2, 1, 3))


def solution(mesh):
    return jax.shard_map(
        functools.partial(shards, mesh.shape["lev"], mesh.shape["lat"]),
        mesh=mesh,
        in_specs=(
            P(None, "lev", "lat", None),
            P("lev", "lat", None),
            P("lev", "lat", None),
            P("lev", "lat", None),
            P("lev", "lat", None),
            P(),
            P(),
            P(),
            P("lev", None),
        ),
        out_specs=P(None, "lev", "lat", None),
        check_vma=False,
    )
```

```python
import functools

import jax
import jax.numpy as jnp
from jax import lax
from jax.experimental import pallas as pl
from jax.experimental.pallas import tpu as pltpu
from jax.sharding import PartitionSpec as P

MESH = pl.DeviceIdType.MESH
CHEM_DT = 0.5
LANES = 128
GROUPS = 6
LAG = 4
REACH = 4
UNIT = 16

F32, BF16 = jnp.float32, jnp.bfloat16


def minmod(a, b):
    zero = jnp.zeros((), a.dtype)
    return jnp.maximum(jnp.minimum(a, b), jnp.minimum(jnp.maximum(a, b), zero))


def face(c, w, lower, upper, lower_slope, upper_slope):
    slope = w * jnp.where(w > 0, lower_slope, upper_slope)
    return c * (jnp.where(c > 0.0, lower, upper) + slope.astype(F32))


def lane_iota():
    return lax.broadcasted_iota(jnp.int32, (UNIT, LANES), 1)


def from_west(chunks):
    rolled = [pltpu.roll(x, 1, 1) for x in chunks]
    first = lane_iota() == 0
    return [jnp.where(first, rolled[k - 1], rolled[k]) for k in range(len(chunks))]


def from_east(chunks):
    rolled = [pltpu.roll(x, LANES - 1, 1) for x in chunks]
    last = lane_iota() == LANES - 1
    n = len(chunks)
    return [jnp.where(last, rolled[(k + 1) % n], rolled[k]) for k in range(n)]


def east_sweep(f, c, w, inv):
    fm = from_west(f)
    d = [a.astype(BF16) - b.astype(BF16) for a, b in zip(f, fm)]
    s = [minmod(a, b) for a, b in zip(from_east(d), d)]
    sm = from_west(s)
    g = [face(*args) for args in zip(c, w, fm, f, sm, s)]
    return [a - inv * (up - lo) for a, up, lo in zip(f, from_east(g), g)]


def roll_pairs(x, shift):
    return jnp.concatenate([pltpu.roll(x[:8], shift, 0), pltpu.roll(x[8:], shift, 0)], axis=0)


def vertical_sweep(below, own, above, c_lo, w_lo, c_hi, w_hi, even):
    f = own.astype(F32)
    m1 = jnp.where(even, roll_pairs(below.astype(F32), 7), roll_pairs(f, 1))
    p1 = jnp.where(even, roll_pairs(f, 7), roll_pairs(above.astype(F32), 1))
    m1b, p1b = m1.astype(BF16), p1.astype(BF16)
    d1, d2, d3, d4 = m1b - below, own - m1b, p1b - own, above - p1b
    sm, s0, sp = minmod(d1, d2), minmod(d2, d3), minmod(d3, d4)
    return f - (face(c_hi, w_hi, f, p1, s0, sp) - face(c_lo, w_lo, m1, f, sm, s0))


def kernel(
    n_lev,
    n_lat,
    x_ref,
    lw_ref,
    ew_ref,
    nw_ref,
    ph_ref,
    rate_ref,
    loss_ref,
    steps_ref,
    slots_ref,
    h_ref,
    keep,
    pd,
    rates_ref,
    below,
    above,
    a_ref,
    send,
    halo,
    lw_next,
    ew_south,
    ew_north,
    nw_south,
    nw_north,
    cv_lo,
    wv_lo,
    cv_hi,
    wv_hi,
    ce,
    be,
    he,
    we2,
    cn,
    bn,
    hn,
    wn2,
    columns,
    lev_send,
    lev_recv,
    lat_send,
    lat_recv,
    wind_send,
    wind_recv,
):
    rows, pairs, lon = h_ref.shape
    span = pairs // GROUPS
    units = span // UNIT
    chunks = lon // LANES
    lev, lat = lax.axis_index("lev"), lax.axis_index("lat")
    up, down = lax.rem(lev + 1, n_lev), lax.rem(lev + n_lev - 1, n_lev)
    north, south = lax.rem(lat + 1, n_lat), lax.rem(lat + n_lat - 1, n_lat)
    has_up, has_down = lev < n_lev - 1, lev > 0
    has_north, has_south = lat < n_lat - 1, lat > 0

    barrier = pltpu.get_barrier_semaphore()
    for to in ((up, lat), (down, lat), (lev, north), (lev, south)):
        pl.semaphore_signal(barrier, inc=1, device_id=to, device_id_type=MESH)

    def lane(k):
        return pl.ds(k * LANES, LANES)

    def remote(src, dst, send_sem, recv_sem, to):
        return pltpu.make_async_remote_copy(
            src_ref=src,
            dst_ref=dst,
            send_sem=send_sem,
            recv_sem=recv_sem,
            device_id=to,
            device_id_type=MESH,
        )

    def wind_copies():
        def wind(n, can_send, can_recv, src, dst, to):
            return can_send, can_recv, remote(src, dst, wind_send.at[n], wind_recv.at[n], to)

        return (
            wind(0, has_down, has_up, lw_ref, lw_next, (down, lat)),
            wind(1, has_south, has_north, ew_ref, ew_north, (lev, south)),
            wind(2, has_north, has_south, ew_ref, ew_south, (lev, north)),
            wind(3, has_south, has_north, nw_ref, nw_north, (lev, south)),
            wind(4, has_north, has_south, nw_ref, nw_south, (lev, north)),
        )

    def members(group):
        return pl.ds(group * span, span)

    def lev_copy(direction, group):
        to = ((up, lat), (down, lat))[direction]
        where = pl.ds(0, rows), members(group)
        return remote(
            x_ref.at[where],
            (below, above)[direction].at[where],
            lev_send.at[direction, group],
            lev_recv.at[direction, group],
            to,
        )

    def lat_copy(direction, group):
        to = ((lev, south), (lev, north))[direction]
        first_row = (0, rows - REACH)[direction]
        return remote(
            send.at[pl.ds(first_row, REACH), members(group)],
            halo.at[pl.ds(REACH * direction, REACH), members(group)],
            lat_send.at[direction, group],
            lat_recv.at[direction, group],
            to,
        )

    lev_can_send, lev_can_recv = (has_up, has_down), (has_down, has_up)
    lat_can_send, lat_can_recv = (has_south, has_north), (has_north, has_south)

    pl.semaphore_wait(barrier, 4)
    for group in range(GROUPS):
        for direction in range(2):

            @pl.when(lev_can_send[direction])
            def _():
                lev_copy(direction, group).start()

        if group == 0:
            for can_send, _, copy in wind_copies():

                @pl.when(can_send)
                def _():
                    copy.start()

    even8 = lax.broadcasted_iota(jnp.int32, (8, LANES), 0) % 2 == 0
    even = lax.broadcasted_iota(jnp.int32, (UNIT, LANES), 0) % 2 == 0

    def pattern(ref, r):
        v = ref[r].astype(F32)
        return jnp.concatenate([v] * 4, axis=0)

    even_row = lax.broadcasted_iota(jnp.int32, (8, lon), 0) % 2 == 0

    def doubled(value):
        return jnp.concatenate([value, value], axis=0).astype(BF16)

    def north_tables(face, c):
        half = jnp.where(c > 0.0, 0.5, -0.5)
        cn[face] = c
        bn[face] = doubled(c)
        hn[face] = doubled(half)
        wn2[face] = doubled(half - 0.25 * c)

    def east_tables(row, c):
        half = jnp.where(c > 0.0, 0.5, -0.5)
        ce[row] = c
        be[row] = doubled(c)
        he[row] = doubled(half)
        we2[row] = doubled(half - 0.25 * c)

    def tables(r, _):
        c = pattern(nw_ref, r)
        north_tables(r + 2, jnp.where((r == 0) & ~has_south, 0.0, c))
        east_tables(r + 2, pattern(ew_ref, r))
        c = pattern(lw_ref, r)
        c = jnp.where(even_row & ~has_down, 0.0, c)
        cv_lo[r] = c
        wv_lo[r] = doubled(jnp.where(c > 0.0, 0.5, -0.5) - 0.5 * c)
        pd[r] = CHEM_DT * pattern(ph_ref, r)
        return 0

    lax.fori_loop(0, rows, tables, 0)

    pair_of = lax.broadcasted_iota(jnp.int32, (pairs, pairs // 2), 0) // 2
    tracer_of = lax.broadcasted_iota(jnp.int32, (pairs, pairs // 2), 1)
    picks = pair_of == tracer_of

    def column(row):
        value = jnp.sum(jnp.where(picks, row, 0.0), axis=1, keepdims=True)
        return jnp.broadcast_to(value, (pairs, LANES))

    steps = steps_ref[...]
    carried = slots_ref[...] >= 0
    first = jnp.where(carried, jnp.where(steps > 1, 0.5, 1.0), 0.0)
    second = jnp.where(carried & (steps > 1), 0.5, 0.0)
    columns[0] = column(first)
    columns[1] = column(second)
    columns[2] = column(loss_ref[...])
    expand = picks.astype(BF16)
    spread = lax.dot_general(
        expand, rate_ref[...], (((1,), (1,)), ((), ())), preferred_element_type=F32
    ).astype(BF16)
    spread = lax.dot_general(
        spread, expand, (((1,), (1,)), ((), ())), preferred_element_type=F32
    )
    same = (
        lax.broadcasted_iota(jnp.int32, (pairs, pairs), 0) % 2
        == lax.broadcasted_iota(jnp.int32, (pairs, pairs), 1) % 2
    )
    rates_ref[...] = jnp.where(same, spread, 0.0).astype(BF16)

    def all_units(body):
        lax.fori_loop(0, rows * (pairs // UNIT), body, 0)

    def halves(value):
        return value[:8], value[8:]

    @pl.when(~has_down)
    def _():
        def fill(i, _):
            r, at = i // (pairs // UNIT), pl.ds(pl.multiple_of(i % (pairs // UNIT) * UNIT, UNIT), UNIT)
            for k in range(chunks):
                here = r, at, lane(k)
                parts = [
                    jnp.where(even8, v, pltpu.roll(v, 1, 0)) for v in halves(x_ref[here].astype(F32))
                ]
                below[here] = jnp.concatenate(parts, axis=0).astype(BF16)
            return 0

        all_units(fill)

    @pl.when(~has_up)
    def _():
        def fill(i, _):
            r, at = i // (pairs // UNIT), pl.ds(pl.multiple_of(i % (pairs // UNIT) * UNIT, UNIT), UNIT)
            for k in range(chunks):
                here = r, at, lane(k)
                parts = [
                    jnp.where(even8, pltpu.roll(v, 7, 0), v) for v in halves(x_ref[here].astype(F32))
                ]
                above[here] = jnp.concatenate(parts, axis=0).astype(BF16)
            return 0

        all_units(fill)
        lw_next[...] = jnp.zeros(lw_next.shape, BF16)

    for at_edge, where, wind in ((~has_north, 0, (ew_north, nw_north)), (~has_south, REACH, (ew_south, nw_south))):

        @pl.when(at_edge)
        def _():
            halo[pl.ds(where, REACH)] = jnp.zeros((REACH, pairs, lon), BF16)
            for ref in wind:
                ref[...] = jnp.zeros(ref.shape, BF16)

    def loss_table(r, _):
        photo = jnp.concatenate([pd[r]] * (pairs // 8), axis=0)
        for k in range(chunks):
            part = pl.ds(k * LANES, LANES)
            keep[r, :, part] = 1.0 / (1.0 + photo[:, k * LANES : (k + 1) * LANES] * columns[2])
        return 0

    lax.fori_loop(0, rows, loss_table, 0)

    for _, can_recv, copy in wind_copies():

        @pl.when(can_recv)
        def _():
            copy.wait_recv()

    def more_tables(r, _):
        mine, theirs = pattern(lw_ref, r), pattern(lw_next, r)
        c = jnp.where(even_row, pltpu.roll(mine, 7, 0), pltpu.roll(theirs, 1, 0))
        c = jnp.where(~even_row & ~has_up, 0.0, c)
        cv_hi[r] = c
        wv_hi[r] = doubled(jnp.where(c > 0.0, 0.5, -0.5) - 0.5 * c)
        return 0

    lax.fori_loop(0, rows, more_tables, 0)

    for r in range(2):
        east_tables(r, pattern(ew_south, rows - 2 + r))
        east_tables(rows + 2 + r, pattern(ew_north, r))
        north_tables(r, pattern(nw_south, rows - 2 + r))
    for r in range(3):
        north_tables(rows + 2 + r, pattern(nw_north, r))

    def column_of(which, at):
        return columns[which, at, :]

    def both(ref, i, k):
        value = ref[i, :, lane(k)]
        return jnp.concatenate([value, value], axis=0)

    def first_sweeps(group, r, unit):
        at = pl.ds(group * span + unit * UNIT, UNIT)
        swept = []
        for k in range(chunks):
            here = r, at, lane(k)
            moved = vertical_sweep(
                below[here],
                x_ref[here],
                above[here],
                both(cv_lo, r, k),
                wv_lo[r, :, lane(k)],
                both(cv_hi, r, k),
                wv_hi[r, :, lane(k)],
                even,
            )
            swept.append(moved.astype(BF16).astype(F32))
        inv = column_of(0, at)
        scale = (0.5 * inv).astype(BF16)
        c = [both(ce, r + 2, k) for k in range(chunks)]
        w = [he[r + 2, :, lane(k)] - scale * be[r + 2, :, lane(k)] for k in range(chunks)]
        result = east_sweep(swept, c, w, inv)
        for k in range(chunks):
            a_ref[r, at, lane(k)] = result[k]
            send[r, at, lane(k)] = result[k].astype(BF16)

    def early(group):
        for direction in range(2):

            @pl.when(lev_can_recv[direction])
            def _():
                lev_copy(direction, group).wait_recv()

        for unit in range(units):
            for r in range(rows):
                first_sweeps(group, r, unit)
        for direction in range(2):

            @pl.when(lat_can_send[direction])
            def _():
                lat_copy(direction, group).start()

    def north_sweep(f, first_face, k, w_of, inv):
        count = len(f) - 4
        b = [v.astype(BF16) for v in f]
        d = [hi - lo for lo, hi in zip(b, b[1:])]
        south_edge, north_edge = 2 - first_face + 1, rows + 2 - first_face + 1
        zero = jnp.zeros((UNIT, LANES), BF16)
        d[south_edge] = jnp.where(has_south, d[south_edge], zero)
        d[north_edge] = jnp.where(has_north, d[north_edge], zero)
        s = [None] + [minmod(lo, hi) for lo, hi in zip(d, d[1:])]
        g = [
            face(both(cn, first_face + i, k), w_of(first_face + i, k), f[i + 1], f[i + 2], s[i + 1], s[i + 2])
            for i in range(count + 1)
        ]
        return [f[i + 2] - inv * (g[i + 1] - g[i]) for i in range(count)]

    def late_sweeps(group, unit):
        at = pl.ds(group * span + unit * UNIT, UNIT)
        inv = column_of(0, at)
        scale = (0.5 * inv).astype(BF16)
        swept = []
        for k in range(chunks):
            f = [halo[REACH + i, at, lane(k)].astype(F32) for i in range(REACH)]
            f += [a_ref[r, at, lane(k)] for r in range(rows)]
            f += [halo[i, at, lane(k)].astype(F32) for i in range(REACH)]
            swept.append(
                north_sweep(f, 0, k, lambda i, k: hn[i, :, lane(k)] - scale * bn[i, :, lane(k)], inv)
            )
        inv = column_of(1, at)
        for r in range(rows + 4):
            c = [both(ce, r, k) for k in range(chunks)]
            w = [we2[r, :, lane(k)] for k in range(chunks)]
            row = east_sweep([swept[k][r] for k in range(chunks)], c, w, inv)
            for k in range(chunks):
                swept[k][r] = row[k]
        for k in range(chunks):
            result = north_sweep(swept[k], 2, k, lambda i, k: wn2[i, :, lane(k)], inv)
            for r in range(rows):
                h_ref[r, at, lane(k)] = result[r].astype(BF16)

    def late(group):
        for direction in range(2):

            @pl.when(lat_can_recv[direction])
            def _():
                lat_copy(direction, group).wait_recv()

        for unit in range(units):
            late_sweeps(group, unit)

    for step in range(GROUPS + LAG):
        if step < GROUPS:
            early(step)
        if step >= LAG:
            late(step - LAG)

    for can_send, _, copy in wind_copies():

        @pl.when(can_send)
        def _():
            copy.wait_send()

    for group in range(GROUPS):
        for direction in range(2):

            @pl.when(lev_can_send[direction])
            def _():
                lev_copy(direction, group).wait_send()

            @pl.when(lat_can_send[direction])
            def _():
                lat_copy(direction, group).wait_send()


def chemistry(h_ref, keep, pd, rates_ref, out_ref, y_ref, out_sem):
    rows, pairs, lon = h_ref.shape
    copies = []
    for r in range(rows):
        values = h_ref[r]
        production = jnp.dot(rates_ref[...], values, preferred_element_type=F32)
        photo = jnp.concatenate([pd[r]] * (pairs // 8), axis=0)
        updated = ((values.astype(F32) + photo * production) * keep[r]).astype(BF16)
        y_ref.reshape(rows, pairs, lon)[r] = updated
        copy = pltpu.make_async_copy(y_ref.at[r], out_ref.at[:, r], out_sem.at[r])
        copy.start()
        copies.append(copy)
    for copy in copies:
        copy.wait()


def shards(
    n_lev,
    n_lat,
    tracer_mass,
    level_wind,
    east_wind,
    north_wind,
    photolysis,
    rate_matrix,
    loss_rate,
    substeps,
    slot_table,
):
    tracers, levels, rows, lon = tracer_mass.shape
    pairs = tracers * levels

    def by_row(wind):
        return jnp.transpose(wind, (1, 0, 2))

    vmem = pl.BlockSpec(memory_space=pltpu.VMEM)
    hbm = pl.BlockSpec(memory_space=pltpu.HBM)
    field = pltpu.VMEM((rows, pairs, lon), F32)
    wind = pltpu.VMEM((rows, levels, lon), BF16)

    def wide(count):
        return pltpu.VMEM((count, 8, lon), F32)

    def twice(count):
        return pltpu.VMEM((count, UNIT, lon), BF16)

    half = pltpu.VMEM((rows, pairs, lon), BF16)
    slabs = pltpu.VMEM((rows, tracers, levels, lon), BF16)
    dma = pltpu.SemaphoreType.DMA
    moved, keep, photo, rates = pl.pallas_call(
        functools.partial(kernel, n_lev, n_lat),
        out_shape=[
            jax.ShapeDtypeStruct((rows, pairs, lon), BF16),
            jax.ShapeDtypeStruct((rows, pairs, lon), F32),
            jax.ShapeDtypeStruct((rows, 8, lon), F32),
            jax.ShapeDtypeStruct((pairs, pairs), BF16),
        ],
        in_specs=[vmem] * 9,
        out_specs=[vmem] * 4,
        scratch_shapes=[
            half,
            half,
            field,
            half,
            pltpu.VMEM((2 * REACH, pairs, lon), BF16),
            wind,
            wind,
            wind,
            wind,
            wind,
            wide(rows),
            twice(rows),
            wide(rows),
            twice(rows),
            wide(rows + 4),
            twice(rows + 4),
            twice(rows + 4),
            twice(rows + 4),
            wide(rows + 5),
            twice(rows + 5),
            twice(rows + 5),
            twice(rows + 5),
            pltpu.VMEM((3, pairs, LANES), F32),
            dma((2, GROUPS)),
            dma((2, GROUPS)),
            dma((2, GROUPS)),
            dma((2, GROUPS)),
            dma((5,)),
            dma((5,)),
        ],
        compiler_params=pltpu.CompilerParams(
            collective_id=0, has_side_effects=True, vmem_limit_bytes=32 * 1024 * 1024
        ),
        name="transport",
    )(
        jnp.transpose(tracer_mass, (2, 0, 1, 3)).reshape(rows, pairs, lon),
        by_row(level_wind),
        by_row(east_wind),
        by_row(north_wind),
        by_row(photolysis),
        rate_matrix,
        loss_rate.reshape(1, tracers),
        substeps.reshape(1, tracers),
        slot_table,
    )
    updated = pl.pallas_call(
        chemistry,
        out_shape=jax.ShapeDtypeStruct((tracers, rows, levels, lon), BF16),
        in_specs=[vmem] * 4,
        out_specs=hbm,
        scratch_shapes=[slabs, dma((rows,))],
        compiler_params=pltpu.CompilerParams(vmem_limit_bytes=16 * 1024 * 1024),
        name="chemistry",
    )(moved, keep, photo, rates)
    return jnp.transpose(updated, (0, 2, 1, 3))


def solution(mesh):
    return jax.shard_map(
        functools.partial(shards, mesh.shape["lev"], mesh.shape["lat"]),
        mesh=mesh,
        in_specs=(
            P(None, "lev", "lat", None),
            P("lev", "lat", None),
            P("lev", "lat", None),
            P("lev", "lat", None),
            P("lev", "lat", None),
            P(),
            P(),
            P(),
            P("lev", None),
        ),
        out_specs=P(None, "lev", "lat", None),
        check_vma=False,
    )
```

```python
import functools

import jax
import jax.numpy as jnp
from jax import lax
from jax.experimental import pallas as pl
from jax.experimental.pallas import tpu as pltpu
from jax.sharding import PartitionSpec as P

MESH = pl.DeviceIdType.MESH
CHEM_DT = 0.5
LANES = 128
GROUPS = 6
LAG = 4
REACH = 4
UNIT = 16

F32, BF16 = jnp.float32, jnp.bfloat16


def minmod(a, b):
    zero = jnp.zeros((), a.dtype)
    return jnp.maximum(jnp.minimum(a, b), jnp.minimum(jnp.maximum(a, b), zero))


def face(c, w, lower, upper, lower_slope, upper_slope):
    slope = w * jnp.where(w > 0, lower_slope, upper_slope)
    return c * (jnp.where(c > 0.0, lower, upper) + slope.astype(F32))


def lane_iota():
    return lax.broadcasted_iota(jnp.int32, (UNIT, LANES), 1)


def from_west(chunks):
    rolled = [pltpu.roll(x, 1, 1) for x in chunks]
    first = lane_iota() == 0
    return [jnp.where(first, rolled[k - 1], rolled[k]) for k in range(len(chunks))]


def from_east(chunks):
    rolled = [pltpu.roll(x, LANES - 1, 1) for x in chunks]
    last = lane_iota() == LANES - 1
    n = len(chunks)
    return [jnp.where(last, rolled[(k + 1) % n], rolled[k]) for k in range(n)]


def east_sweep(f, c, w, inv):
    fm = from_west(f)
    d = [a.astype(BF16) - b.astype(BF16) for a, b in zip(f, fm)]
    s = [minmod(a, b) for a, b in zip(from_east(d), d)]
    sm = from_west(s)
    g = [face(*args) for args in zip(c, w, fm, f, sm, s)]
    return [a - inv * (up - lo) for a, up, lo in zip(f, from_east(g), g)]


def roll_pairs(x, shift):
    return jnp.concatenate([pltpu.roll(x[:8], shift, 0), pltpu.roll(x[8:], shift, 0)], axis=0)


def vertical_sweep(below, own, above, c_lo, w_lo, c_hi, w_hi, even):
    f = own.astype(F32)
    m1 = jnp.where(even, roll_pairs(below.astype(F32), 7), roll_pairs(f, 1))
    p1 = jnp.where(even, roll_pairs(f, 7), roll_pairs(above.astype(F32), 1))
    m1b, p1b = m1.astype(BF16), p1.astype(BF16)
    d1, d2, d3, d4 = m1b - below, own - m1b, p1b - own, above - p1b
    sm, s0, sp = minmod(d1, d2), minmod(d2, d3), minmod(d3, d4)
    return f - (face(c_hi, w_hi, f, p1, s0, sp) - face(c_lo, w_lo, m1, f, sm, s0))


def kernel(
    n_lev,
    n_lat,
    x_ref,
    lw_ref,
    ew_ref,
    nw_ref,
    ph_ref,
    rate_ref,
    loss_ref,
    steps_ref,
    slots_ref,
    h_ref,
    keep,
    pd,
    rates_ref,
    below,
    above,
    a_ref,
    send,
    halo,
    lw_next,
    ew_south,
    ew_north,
    nw_south,
    nw_north,
    cv_lo,
    wv_lo,
    cv_hi,
    wv_hi,
    ce,
    be,
    he,
    we2,
    cn,
    bn,
    hn,
    wn2,
    columns,
    lev_send,
    lev_recv,
    lat_send,
    lat_recv,
    wind_send,
    wind_recv,
):
    rows, pairs, lon = h_ref.shape
    span = pairs // GROUPS
    units = span // UNIT
    chunks = lon // LANES
    lev, lat = lax.axis_index("lev"), lax.axis_index("lat")
    up, down = lax.rem(lev + 1, n_lev), lax.rem(lev + n_lev - 1, n_lev)
    north, south = lax.rem(lat + 1, n_lat), lax.rem(lat + n_lat - 1, n_lat)
    has_up, has_down = lev < n_lev - 1, lev > 0
    has_north, has_south = lat < n_lat - 1, lat > 0

    barrier = pltpu.get_barrier_semaphore()
    for to in ((up, lat), (down, lat), (lev, north), (lev, south)):
        pl.semaphore_signal(barrier, inc=1, device_id=to, device_id_type=MESH)

    def lane(k):
        return pl.ds(k * LANES, LANES)

    def remote(src, dst, send_sem, recv_sem, to):
        return pltpu.make_async_remote_copy(
            src_ref=src,
            dst_ref=dst,
            send_sem=send_sem,
            recv_sem=recv_sem,
            device_id=to,
            device_id_type=MESH,
        )

    def wind_copies():
        def wind(n, can_send, can_recv, src, dst, to):
            return can_send, can_recv, remote(src, dst, wind_send.at[n], wind_recv.at[n], to)

        return (
            wind(0, has_down, has_up, lw_ref, lw_next, (down, lat)),
            wind(1, has_south, has_north, ew_ref, ew_north, (lev, south)),
            wind(2, has_north, has_south, ew_ref, ew_south, (lev, north)),
            wind(3, has_south, has_north, nw_ref, nw_north, (lev, south)),
            wind(4, has_north, has_south, nw_ref, nw_south, (lev, north)),
        )

    def members(group):
        return pl.ds(group * span, span)

    def lev_copy(direction, group):
        to = ((up, lat), (down, lat))[direction]
        where = pl.ds(0, rows), members(group)
        return remote(
            x_ref.at[where],
            (below, above)[direction].at[where],
            lev_send.at[direction, group],
            lev_recv.at[direction, group],
            to,
        )

    def lat_copy(direction, group):
        to = ((lev, south), (lev, north))[direction]
        first_row = (0, rows - REACH)[direction]
        return remote(
            send.at[pl.ds(first_row, REACH), members(group)],
            halo.at[pl.ds(REACH * direction, REACH), members(group)],
            lat_send.at[direction, group],
            lat_recv.at[direction, group],
            to,
        )

    lev_can_send, lev_can_recv = (has_up, has_down), (has_down, has_up)
    lat_can_send, lat_can_recv = (has_south, has_north), (has_north, has_south)

    pl.semaphore_wait(barrier, 4)
    for can_send, _, copy in wind_copies():

        @pl.when(can_send)
        def _():
            copy.start()

    for group in range(GROUPS):
        for direction in range(2):

            @pl.when(lev_can_send[direction])
            def _():
                lev_copy(direction, group).start()

    even8 = lax.broadcasted_iota(jnp.int32, (8, LANES), 0) % 2 == 0
    even = lax.broadcasted_iota(jnp.int32, (UNIT, LANES), 0) % 2 == 0

    def pattern(ref, r):
        v = ref[r].astype(F32)
        return jnp.concatenate([v] * 4, axis=0)

    even_row = lax.broadcasted_iota(jnp.int32, (8, lon), 0) % 2 == 0

    def doubled(value):
        return jnp.concatenate([value, value], axis=0).astype(BF16)

    def north_tables(face, c):
        half = jnp.where(c > 0.0, 0.5, -0.5)
        cn[face] = c
        bn[face] = doubled(c)
        hn[face] = doubled(half)
        wn2[face] = doubled(half - 0.25 * c)

    def east_tables(row, c):
        half = jnp.where(c > 0.0, 0.5, -0.5)
        ce[row] = c
        be[row] = doubled(c)
        he[row] = doubled(half)
        we2[row] = doubled(half - 0.25 * c)

    def tables(r, _):
        c = pattern(nw_ref, r)
        north_tables(r + 2, jnp.where((r == 0) & ~has_south, 0.0, c))
        east_tables(r + 2, pattern(ew_ref, r))
        c = pattern(lw_ref, r)
        c = jnp.where(even_row & ~has_down, 0.0, c)
        cv_lo[r] = c
        wv_lo[r] = doubled(jnp.where(c > 0.0, 0.5, -0.5) - 0.5 * c)
        pd[r] = CHEM_DT * pattern(ph_ref, r)
        return 0

    lax.fori_loop(0, rows, tables, 0)

    pair_of = lax.broadcasted_iota(jnp.int32, (pairs, pairs // 2), 0) // 2
    tracer_of = lax.broadcasted_iota(jnp.int32, (pairs, pairs // 2), 1)
    picks = pair_of == tracer_of

    def column(row):
        value = jnp.sum(jnp.where(picks, row, 0.0), axis=1, keepdims=True)
        return jnp.broadcast_to(value, (pairs, LANES))

    steps = steps_ref[...]
    carried = slots_ref[...] >= 0
    first = jnp.where(carried, jnp.where(steps > 1, 0.5, 1.0), 0.0)
    second = jnp.where(carried & (steps > 1), 0.5, 0.0)
    columns[0] = column(first)
    columns[1] = column(second)
    columns[2] = column(loss_ref[...])
    expand = picks.astype(BF16)
    spread = lax.dot_general(
        expand, rate_ref[...], (((1,), (1,)), ((), ())), preferred_element_type=F32
    ).astype(BF16)
    spread = lax.dot_general(
        spread, expand, (((1,), (1,)), ((), ())), preferred_element_type=F32
    )
    same = (
        lax.broadcasted_iota(jnp.int32, (pairs, pairs), 0) % 2
        == lax.broadcasted_iota(jnp.int32, (pairs, pairs), 1) % 2
    )
    rates_ref[...] = jnp.where(same, spread, 0.0).astype(BF16)

    def all_units(body):
        lax.fori_loop(0, rows * (pairs // UNIT), body, 0)

    def halves(value):
        return value[:8], value[8:]

    @pl.when(~has_down)
    def _():
        def fill(i, _):
            r, at = i // (pairs // UNIT), pl.ds(pl.multiple_of(i % (pairs // UNIT) * UNIT, UNIT), UNIT)
            for k in range(chunks):
                here = r, at, lane(k)
                parts = [
                    jnp.where(even8, v, pltpu.roll(v, 1, 0)) for v in halves(x_ref[here].astype(F32))
                ]
                below[here] = jnp.concatenate(parts, axis=0).astype(BF16)
            return 0

        all_units(fill)

    @pl.when(~has_up)
    def _():
        def fill(i, _):
            r, at = i // (pairs // UNIT), pl.ds(pl.multiple_of(i % (pairs // UNIT) * UNIT, UNIT), UNIT)
            for k in range(chunks):
                here = r, at, lane(k)
                parts = [
                    jnp.where(even8, pltpu.roll(v, 7, 0), v) for v in halves(x_ref[here].astype(F32))
                ]
                above[here] = jnp.concatenate(parts, axis=0).astype(BF16)
            return 0

        all_units(fill)
        lw_next[...] = jnp.zeros(lw_next.shape, BF16)

    for at_edge, where, wind in ((~has_north, 0, (ew_north, nw_north)), (~has_south, REACH, (ew_south, nw_south))):

        @pl.when(at_edge)
        def _():
            halo[pl.ds(where, REACH)] = jnp.zeros((REACH, pairs, lon), BF16)
            for ref in wind:
                ref[...] = jnp.zeros(ref.shape, BF16)

    def loss_table(r, _):
        photo = jnp.concatenate([pd[r]] * (pairs // 8), axis=0)
        for k in range(chunks):
            part = pl.ds(k * LANES, LANES)
            keep[r, :, part] = 1.0 / (1.0 + photo[:, k * LANES : (k + 1) * LANES] * columns[2])
        return 0

    lax.fori_loop(0, rows, loss_table, 0)

    for _, can_recv, copy in wind_copies():

        @pl.when(can_recv)
        def _():
            copy.wait_recv()

    def more_tables(r, _):
        mine, theirs = pattern(lw_ref, r), pattern(lw_next, r)
        c = jnp.where(even_row, pltpu.roll(mine, 7, 0), pltpu.roll(theirs, 1, 0))
        c = jnp.where(~even_row & ~has_up, 0.0, c)
        cv_hi[r] = c
        wv_hi[r] = doubled(jnp.where(c > 0.0, 0.5, -0.5) - 0.5 * c)
        return 0

    lax.fori_loop(0, rows, more_tables, 0)

    for r in range(2):
        east_tables(r, pattern(ew_south, rows - 2 + r))
        east_tables(rows + 2 + r, pattern(ew_north, r))
        north_tables(r, pattern(nw_south, rows - 2 + r))
    for r in range(3):
        north_tables(rows + 2 + r, pattern(nw_north, r))

    def column_of(which, at):
        return columns[which, at, :]

    def both(ref, i, k):
        value = ref[i, :, lane(k)]
        return jnp.concatenate([value, value], axis=0)

    def first_sweeps(group, r, unit):
        at = pl.ds(group * span + unit * UNIT, UNIT)
        swept = []
        for k in range(chunks):
            here = r, at, lane(k)
            moved = vertical_sweep(
                below[here],
                x_ref[here],
                above[here],
                both(cv_lo, r, k),
                wv_lo[r, :, lane(k)],
                both(cv_hi, r, k),
                wv_hi[r, :, lane(k)],
                even,
            )
            swept.append(moved.astype(BF16).astype(F32))
        inv = column_of(0, at)
        scale = (0.5 * inv).astype(BF16)
        c = [both(ce, r + 2, k) for k in range(chunks)]
        w = [he[r + 2, :, lane(k)] - scale * be[r + 2, :, lane(k)] for k in range(chunks)]
        result = east_sweep(swept, c, w, inv)
        for k in range(chunks):
            a_ref[r, at, lane(k)] = result[k]
            send[r, at, lane(k)] = result[k].astype(BF16)

    def early(group):
        for direction in range(2):

            @pl.when(lev_can_recv[direction])
            def _():
                lev_copy(direction, group).wait_recv()

        for unit in range(units):
            for r in range(rows):
                first_sweeps(group, r, unit)
        for direction in range(2):

            @pl.when(lat_can_send[direction])
            def _():
                lat_copy(direction, group).start()

    def north_sweep(f, first_face, k, w_of, inv):
        count = len(f) - 4
        b = [v.astype(BF16) for v in f]
        d = [hi - lo for lo, hi in zip(b, b[1:])]
        south_edge, north_edge = 2 - first_face + 1, rows + 2 - first_face + 1
        zero = jnp.zeros((UNIT, LANES), BF16)
        d[south_edge] = jnp.where(has_south, d[south_edge], zero)
        d[north_edge] = jnp.where(has_north, d[north_edge], zero)
        s = [None] + [minmod(lo, hi) for lo, hi in zip(d, d[1:])]
        g = [
            face(both(cn, first_face + i, k), w_of(first_face + i, k), f[i + 1], f[i + 2], s[i + 1], s[i + 2])
            for i in range(count + 1)
        ]
        return [f[i + 2] - inv * (g[i + 1] - g[i]) for i in range(count)]

    def late_sweeps(group, unit):
        at = pl.ds(group * span + unit * UNIT, UNIT)
        inv = column_of(0, at)
        scale = (0.5 * inv).astype(BF16)
        swept = []
        for k in range(chunks):
            f = [halo[REACH + i, at, lane(k)].astype(F32) for i in range(REACH)]
            f += [a_ref[r, at, lane(k)] for r in range(rows)]
            f += [halo[i, at, lane(k)].astype(F32) for i in range(REACH)]
            swept.append(
                north_sweep(f, 0, k, lambda i, k: hn[i, :, lane(k)] - scale * bn[i, :, lane(k)], inv)
            )
        inv = column_of(1, at)
        for r in range(rows + 4):
            c = [both(ce, r, k) for k in range(chunks)]
            w = [we2[r, :, lane(k)] for k in range(chunks)]
            row = east_sweep([swept[k][r] for k in range(chunks)], c, w, inv)
            for k in range(chunks):
                swept[k][r] = row[k]
        for k in range(chunks):
            result = north_sweep(swept[k], 2, k, lambda i, k: wn2[i, :, lane(k)], inv)
            for r in range(rows):
                h_ref[r, at, lane(k)] = result[r].astype(BF16)

    def late(group):
        for direction in range(2):

            @pl.when(lat_can_recv[direction])
            def _():
                lat_copy(direction, group).wait_recv()

        for unit in range(units):
            late_sweeps(group, unit)

    for step in range(GROUPS + LAG):
        if step < GROUPS:
            early(step)
        if step >= LAG:
            late(step - LAG)

    for can_send, _, copy in wind_copies():

        @pl.when(can_send)
        def _():
            copy.wait_send()

    for group in range(GROUPS):
        for direction in range(2):

            @pl.when(lev_can_send[direction])
            def _():
                lev_copy(direction, group).wait_send()

            @pl.when(lat_can_send[direction])
            def _():
                lat_copy(direction, group).wait_send()


def chemistry(h_ref, keep, pd, rates_ref, out_ref, y_ref, out_sem):
    rows, pairs, lon = h_ref.shape
    copies = []
    for r in range(rows):
        values = h_ref[r]
        production = jnp.dot(rates_ref[...], values, preferred_element_type=F32)
        photo = jnp.concatenate([pd[r]] * (pairs // 8), axis=0)
        updated = ((values.astype(F32) + photo * production) * keep[r]).astype(BF16)
        y_ref.reshape(rows, pairs, lon)[r] = updated
        copy = pltpu.make_async_copy(y_ref.at[r], out_ref.at[:, r], out_sem.at[r])
        copy.start()
        copies.append(copy)
    for copy in copies:
        copy.wait()


def shards(
    n_lev,
    n_lat,
    tracer_mass,
    level_wind,
    east_wind,
    north_wind,
    photolysis,
    rate_matrix,
    loss_rate,
    substeps,
    slot_table,
):
    tracers, levels, rows, lon = tracer_mass.shape
    pairs = tracers * levels

    def by_row(wind):
        return jnp.transpose(wind, (1, 0, 2))

    vmem = pl.BlockSpec(memory_space=pltpu.VMEM)
    hbm = pl.BlockSpec(memory_space=pltpu.HBM)
    field = pltpu.VMEM((rows, pairs, lon), F32)
    wind = pltpu.VMEM((rows, levels, lon), BF16)

    def wide(count):
        return pltpu.VMEM((count, 8, lon), F32)

    def twice(count):
        return pltpu.VMEM((count, UNIT, lon), BF16)

    half = pltpu.VMEM((rows, pairs, lon), BF16)
    slabs = pltpu.VMEM((rows, tracers, levels, lon), BF16)
    dma = pltpu.SemaphoreType.DMA
    moved, keep, photo, rates = pl.pallas_call(
        functools.partial(kernel, n_lev, n_lat),
        out_shape=[
            jax.ShapeDtypeStruct((rows, pairs, lon), BF16),
            jax.ShapeDtypeStruct((rows, pairs, lon), F32),
            jax.ShapeDtypeStruct((rows, 8, lon), F32),
            jax.ShapeDtypeStruct((pairs, pairs), BF16),
        ],
        in_specs=[vmem] * 9,
        out_specs=[vmem] * 4,
        scratch_shapes=[
            half,
            half,
            field,
            half,
            pltpu.VMEM((2 * REACH, pairs, lon), BF16),
            wind,
            wind,
            wind,
            wind,
            wind,
            wide(rows),
            twice(rows),
            wide(rows),
            twice(rows),
            wide(rows + 4),
            twice(rows + 4),
            twice(rows + 4),
            twice(rows + 4),
            wide(rows + 5),
            twice(rows + 5),
            twice(rows + 5),
            twice(rows + 5),
            pltpu.VMEM((3, pairs, LANES), F32),
            dma((2, GROUPS)),
            dma((2, GROUPS)),
            dma((2, GROUPS)),
            dma((2, GROUPS)),
            dma((5,)),
            dma((5,)),
        ],
        compiler_params=pltpu.CompilerParams(
            collective_id=0, has_side_effects=True, vmem_limit_bytes=32 * 1024 * 1024
        ),
        name="transport",
    )(
        jnp.transpose(tracer_mass, (2, 0, 1, 3)).reshape(rows, pairs, lon),
        by_row(level_wind),
        by_row(east_wind),
        by_row(north_wind),
        by_row(photolysis),
        rate_matrix,
        loss_rate.reshape(1, tracers),
        substeps.reshape(1, tracers),
        slot_table,
    )
    updated = pl.pallas_call(
        chemistry,
        out_shape=jax.ShapeDtypeStruct((tracers, rows, levels, lon), BF16),
        in_specs=[vmem] * 4,
        out_specs=hbm,
        scratch_shapes=[slabs, dma((rows,))],
        compiler_params=pltpu.CompilerParams(vmem_limit_bytes=16 * 1024 * 1024),
        name="chemistry",
    )(moved, keep, photo, rates)
    return jnp.transpose(updated, (0, 2, 1, 3))


def solution(mesh):
    return jax.shard_map(
        functools.partial(shards, mesh.shape["lev"], mesh.shape["lat"]),
        mesh=mesh,
        in_specs=(
            P(None, "lev", "lat", None),
            P("lev", "lat", None),
            P("lev", "lat", None),
            P("lev", "lat", None),
            P("lev", "lat", None),
            P(),
            P(),
            P(),
            P("lev", None),
        ),
        out_specs=P(None, "lev", "lat", None),
        check_vma=False,
    )
```
